32 devices in a mesh: node: 8 (over z, y), local: 4 (over x, core).
Axes of the slice: x: 2, y: 2, z: 4, core: 2. Of those that a mesh axis runs over, the one named last changes fastest.
Arguments:
- activations: bfloat16 [8192, 5120], P(('node', 'local')), may hold values from -6 to 6
- queries: bfloat16 [8192, 5120], P(('node', 'local')), may hold values from -100 to 100
- rotated_key_value: bfloat16 [8192, 2048], P(('node', 'local')), may hold values from -5 to 5
- attention_out_grad: bfloat16 [8192, 5120], P(('node', 'local')), may hold values from -6 to 6
- adapter_down: bfloat16 [5120, 128], replicated, may hold values from -0.078125 to 0.078125
- adapter_up: bfloat16 [128, 1024], replicated, may hold values from -0.75 to 0.75
- bin_local_index: int32 [32, 256], P(('node', 'local')), may hold values from 0 to 3, as said below
- bin_row_offset: int32 [32, 256], P(('node', 'local')), may hold values from 0 to 3, as said below
- spill_node: int32 [32, 256], P(('node', 'local')), may hold values from 0 to 7, as said below
- spill_row_offset: int32 [32, 256], P(('node', 'local')), may hold values from 0 to 3, as said below
- arrival_pick_index: int32 [32, 256], P(('node', 'local')), may hold values from 0 to 303, as said below
- packed_sequence_number: int32 [32, 256], P(('node', 'local')), may hold values from 0 to 7, never falling along the last dimension, each value on 1 to 128 neighbouring positions
Outputs:
- key_value_cotangent: bfloat16 [8192, 2048], P(('node', 'local'))
- down_factor_grad: float32 [5120, 128], P(('node', 'local'))
- up_factor_grad_transposed: float32 [1024, 128], P(('node', 'local'))
The draws below stay inside these ranges and needn't reach their ends.
Inputs may be any that keep to these rules, and one draw needn't show every extreme that they name: `bin_local_index`: rows that stay or overflow carry the device's own local index. At most 4 rows of a device go to one other bin of its node, and that bin sends back exactly as many to it; in every node one device sends 4 rows to every other bin of the node. `bin_row_offset`: offsets of the rows one device sends to one bin are 0 up to their count minus 1; zero for other rows. `spill_node`: A row moves across nodes only if it stays in its node's bin of its own local index otherwise; at most 4 rows of a device go to one other node, and as many come back; for every local index one node sends 4 rows to every other node. Rows that do not overflow carry their own node. `spill_row_offset`: offsets of the overflow rows one device sends to one node are 0 up to their count minus 1; zero for other rows. `arrival_pick_index`: every bin holds exactly 256 rows: each row of the arrival list of 304 entries that is filled is named once, and no empty entry is named.
All inputs are finite; a program needn't handle non-finite values.
Results may differ from the reference program's by a relative error of at most 0.0056.
Values may be sent and summed in bfloat16 or wider, within the bound.
A program may use at most 128 MiB of HBM per device.

```python
import math
import jax
import jax.numpy as jnp
import numpy as np
from jax import lax

MODEL_WIDTH = 5120
KV_HEADS = 8
HEAD = 128
ADAPTER_RANK = 64
TOK_DEV = 256
CAP_L = 4
CAP_N = 4
GROUP = 5
QW = 5120
KEY_HEAD_WIDTH = 1024
BINS = 32
TOKENS = 8192
N_NODE = 8
N_LOCAL = 4


def symmetric_counts(seed_key, groups, members, capacity):
    raw_counts = jax.random.randint(jax.random.fold_in(seed_key, 1), (groups, members, members), 0, capacity + 1)
    upper_half = jnp.triu(raw_counts, 1)
    count_table = upper_half + jnp.swapaxes(upper_half, 1, 2)
    full_row = jax.random.randint(jax.random.fold_in(seed_key, 2), (groups, 1, 1), 0, members)
    member_ids = jnp.arange(members)
    hit_mask = (member_ids[None, :, None] == full_row) | (member_ids[None, None, :] == full_row)
    count_table = jnp.where(hit_mask, capacity, count_table)
    return jnp.where(member_ids[:, None] == member_ids[None, :], 0, count_table)


def route_plan(seed_key):
    within = symmetric_counts(jax.random.fold_in(seed_key, 11), N_NODE, N_LOCAL, CAP_L)
    across = symmetric_counts(jax.random.fold_in(seed_key, 12), N_LOCAL, N_NODE, CAP_N)
    device = jnp.arange(BINS)
    dev_node = device // N_LOCAL
    dev_local = device % N_LOCAL
    send_in = within[dev_node, dev_local]
    send_out = across[dev_local, dev_node]
    recv_in = within[dev_node, :, dev_local]
    recv_out = across[dev_local, :, dev_node]
    cum_in = jnp.cumsum(send_in, axis=1)
    cum_out = jnp.cumsum(send_out, axis=1)
    total_in = cum_in[:, -1:]
    total_out = cum_out[:, -1:]
    ticket = jnp.arange(TOK_DEV)[None, :]
    dest_in = jnp.minimum(jnp.sum(cum_in[:, None, :] <= ticket[:, :, None], axis=2), N_LOCAL - 1)
    off_in = ticket - jnp.take_along_axis(cum_in - send_in, dest_in, axis=1)
    later = ticket - total_in
    dest_out = jnp.minimum(jnp.sum(cum_out[:, None, :] <= later[:, :, None], axis=2), N_NODE - 1)
    off_out = later - jnp.take_along_axis(cum_out - send_out, dest_out, axis=1)
    is_in = ticket < total_in
    is_out = (later >= 0) & (later < total_out)
    perms = jax.vmap(lambda row_key: jax.random.permutation(row_key, TOK_DEV))(jax.random.split(jax.random.fold_in(seed_key, 13), BINS))
    of_row = jnp.argsort(perms, axis=1)

    def by_row(values):
        return jnp.take_along_axis(jnp.broadcast_to(values, (BINS, TOK_DEV)), of_row, axis=1)
    row_in = by_row(is_in)
    row_out = by_row(is_out)
    bin_local_index = jnp.where(row_in, by_row(dest_in), dev_local[:, None])
    bin_row_offset = jnp.where(row_in, by_row(off_in), 0)
    spill_node = jnp.where(row_out, by_row(dest_out), dev_node[:, None])
    spill_row_offset = jnp.where(row_out, by_row(off_out), 0)
    stays = jnp.logical_not(row_in | row_out)
    near_valid = (jnp.arange(CAP_L)[None, None, :] < recv_in[:, :, None]).reshape(BINS, N_LOCAL * CAP_L)
    far_valid = (jnp.arange(CAP_N)[None, None, :] < recv_out[:, :, None]).reshape(BINS, N_NODE * CAP_N)
    valid = jnp.concatenate([stays, near_valid, far_valid], axis=1)
    valid_order = jnp.argsort(jnp.where(valid, 0, 1), axis=1, stable=True)[:, :TOK_DEV]
    shuffle = jax.vmap(lambda row_key: jax.random.permutation(row_key, TOK_DEV))(jax.random.split(jax.random.fold_in(seed_key, 14), BINS))
    arrival_pick_index = jnp.take_along_axis(valid_order, shuffle, axis=1)
    return (bin_local_index.astype(jnp.int32), bin_row_offset.astype(jnp.int32), spill_node.astype(jnp.int32), spill_row_offset.astype(jnp.int32), arrival_pick_index.astype(jnp.int32))


def draw_bin_local_index(key, part):
    return route_plan(key)[0]


def draw_bin_row_offset(key, part):
    return route_plan(key)[1]


def draw_spill_node(key, part):
    return route_plan(key)[2]


def draw_spill_row_offset(key, part):
    return route_plan(key)[3]


def draw_arrival_pick_index(key, part):
    return route_plan(key)[4]


def shared_keys(seed_key):
    return jax.random.truncated_normal(jax.random.fold_in(seed_key, 101), -5.0, 5.0, (TOKENS, KEY_HEAD_WIDTH), jnp.float32)


def draw_queries(key, part):
    key = jax.random.fold_in(key, 3)
    result = jax.random.truncated_normal(jax.random.fold_in(key, 1), -5.0, 5.0, (TOKENS, QW), jnp.float32)
    return result.astype(jnp.bfloat16)


def draw_rotated_key_value(key, part):
    key_rows = shared_keys(key)
    key = jax.random.fold_in(key, 5)
    value_rows = jax.random.truncated_normal(jax.random.fold_in(key, 1), -5.0, 5.0, (TOKENS, KEY_HEAD_WIDTH), jnp.float32)
    return jnp.concatenate([key_rows, value_rows], axis=1).astype(jnp.bfloat16)


def shard_levels(own_key, dims, shards, smallest, top_value):
    def one(dim, parts):
        heights = jax.random.uniform(jax.random.fold_in(jax.random.fold_in(own_key, 6), dim), (parts,), jnp.float32, smallest / len(shards), top_value / len(shards))
        return jnp.repeat(jnp.exp(heights), dims[dim] // parts).reshape((-1,) + (1,) * (len(dims) - dim - 1))

    level = one(*shards[0])
    for cut in shards[1:]:
        level = level * one(*cut)
    return level


def profile(number_of, total, bound, lean):
    weights = [(1 << 20) // math.isqrt(rank ** lean) + 1 for rank in range(2, number_of + 1)]
    rest, counts = total - bound - (number_of - 1), [1] * (number_of - 1)
    while rest > 0:
        candidates = [i for i in range(number_of - 1) if counts[i] < bound]
        mass, remaining = sum([weights[i] for i in candidates]), rest
        for i in candidates:
            more = min(bound - counts[i], max(1, remaining * weights[i] // mass), rest)
            counts[i] = counts[i] + more
            rest = rest - more
    return np.array([bound] + counts)


def uneven_parts(stream_key, count, total, bound, lean):
    if count == 2:
        one = jax.random.randint(stream_key, (), max(1, total - bound), min(bound, total - 1) + 1)
        return jnp.stack([one, total - one])
    sizes = jnp.asarray(profile(count, total, bound, lean), jnp.int32)
    twos = (count - 1) // 2
    giver, taker = sizes[1:1 + 2 * twos:2], sizes[2:2 + 2 * twos:2]
    slack = jnp.minimum(giver - 1, bound - taker)
    passed = jax.random.randint(jax.random.fold_in(stream_key, 1), (twos,), 0, 1 << 20) % (slack + 1)
    sizes = sizes.at[1:1 + 2 * twos:2].set(giver - passed).at[2:2 + 2 * twos:2].set(taker + passed)
    return sizes[jax.random.permutation(jax.random.fold_in(stream_key, 2), count)]


def scatter_about(own_key, dims, deviation, reach, cuts=(), kind=jnp.bfloat16):
    gain = shard_levels(own_key, dims, cuts, -0.22, 0.18) if cuts else 1.0
    array = jax.random.normal(own_key, dims, jnp.float32) * deviation * gain
    return jnp.minimum(jnp.maximum(array, -reach), reach).astype(kind)


def setup_inputs(seed: int = 0) -> dict:
    seeds = jax.random.split(jax.random.key(seed), 13)
    activations = scatter_about(seeds[0], (TOKENS, MODEL_WIDTH), 1.0, 6.0, ((0, 32),))
    queries = draw_queries(jax.random.fold_in(seeds[12], 71), 0)
    rotated_key_value = draw_rotated_key_value(jax.random.fold_in(seeds[12], 71), 0)
    attention_out_grad = scatter_about(seeds[3], (TOKENS, QW), 1.0, 6.0, ((0, 32),))
    adapter_down = scatter_about(seeds[4], (MODEL_WIDTH, 2 * ADAPTER_RANK), MODEL_WIDTH ** -0.5, 0.078125)
    adapter_up = scatter_about(seeds[5], (2 * ADAPTER_RANK, KEY_HEAD_WIDTH), ADAPTER_RANK ** -0.5, 0.75)
    bin_local_index = draw_bin_local_index(jax.random.fold_in(seeds[12], 71), 0)
    bin_row_offset = draw_bin_row_offset(jax.random.fold_in(seeds[12], 71), 0)
    spill_node = draw_spill_node(jax.random.fold_in(seeds[12], 71), 0)
    spill_row_offset = draw_spill_row_offset(jax.random.fold_in(seeds[12], 71), 0)
    arrival_pick_index = draw_arrival_pick_index(jax.random.fold_in(seeds[12], 71), 0)
    packed_sequence_number = jax.vmap(lambda own: jnp.searchsorted(jnp.cumsum(uneven_parts(own, 8, TOK_DEV, TOK_DEV // 2, 2)), jnp.arange(TOK_DEV), side="right"))(jax.random.split(seeds[11], BINS)).reshape((BINS, TOK_DEV)).astype(jnp.int32)
    return {"activations": activations, "queries": queries, "rotated_key_value": rotated_key_value, "attention_out_grad": attention_out_grad, "adapter_down": adapter_down, "adapter_up": adapter_up, "bin_local_index": bin_local_index, "bin_row_offset": bin_row_offset, "spill_node": spill_node, "spill_row_offset": spill_row_offset, "arrival_pick_index": arrival_pick_index, "packed_sequence_number": packed_sequence_number}


rope_theta = 1000000.0

def rope_tables(segments):
    slot_ids = jnp.arange(segments.shape[0], dtype=jnp.int32)
    seg_start = lax.optimization_barrier(jnp.sum((segments[None, :] < segments[:, None]).astype(jnp.int32), axis=1))
    position = (slot_ids - seg_start).astype(jnp.float32)
    frequency = rope_theta ** (-jnp.arange(0, HEAD, 2).astype(jnp.float32) / HEAD)
    angles = position[:, None] * frequency[None, :]
    return (jnp.cos(angles), jnp.sin(angles))

def unrotate(key_rot, cosine_table, sine_table):
    half_head = HEAD // 2
    first_half = key_rot[..., :half_head]
    second_half = key_rot[..., half_head:]
    cos_rows = cosine_table[:, None, :]
    sin_rows = sine_table[:, None, :]
    return jnp.concatenate([first_half * cos_rows + second_half * sin_rows, second_half * cos_rows - first_half * sin_rows], axis=-1)

def bin_backward(query_rows, kv_rows, grad_rows, segments):
    row_count = query_rows.shape[0]
    score_scale = 1.0 / jnp.sqrt(jnp.float32(HEAD))
    slot_ids = jnp.arange(row_count, dtype=jnp.int32)
    allowed = (segments[:, None] == segments[None, :]) & (slot_ids[None, :] <= slot_ids[:, None])
    query_heads = query_rows.astype(jnp.float32).reshape(row_count, KV_HEADS, GROUP, HEAD)
    grad_heads = grad_rows.astype(jnp.float32).reshape(row_count, KV_HEADS, GROUP, HEAD)
    key_part = kv_rows[:, :KEY_HEAD_WIDTH].astype(jnp.float32).reshape(row_count, KV_HEADS, HEAD)
    value_part = kv_rows[:, KEY_HEAD_WIDTH:].astype(jnp.float32).reshape(row_count, KV_HEADS, HEAD)
    scores = jnp.einsum('igsd,jgd->gsij', query_heads, key_part) * score_scale
    scores = jnp.where(allowed[None, None], scores, -jnp.inf)
    row_max = lax.optimization_barrier(jnp.max(scores, axis=-1, keepdims=True))
    weights = jnp.exp(scores - row_max)
    probs = weights / lax.optimization_barrier(jnp.sum(weights, axis=-1, keepdims=True))
    prob_grad = jnp.einsum('igsd,jgd->gsij', grad_heads, value_part)
    row_delta = lax.optimization_barrier(jnp.sum(probs * prob_grad, axis=-1, keepdims=True))
    score_grad = (probs * (prob_grad - row_delta)).astype(jnp.bfloat16)
    probs_low = probs.astype(jnp.bfloat16)
    probs_back = lax.optimization_barrier(probs_low).astype(jnp.float32)
    score_back = lax.optimization_barrier(score_grad).astype(jnp.float32)
    value_cotangent_rows = jnp.einsum('gsij,igsd->jgd', probs_back, grad_heads)
    key_rot = jnp.einsum('gsij,igsd->jgd', score_back, query_heads) * score_scale
    cosine_table, sine_table = rope_tables(segments)
    key_cotangent_rows = unrotate(key_rot, cosine_table, sine_table)
    return jnp.concatenate([key_cotangent_rows.reshape(row_count, KEY_HEAD_WIDTH), value_cotangent_rows.reshape(row_count, KEY_HEAD_WIDTH)], axis=1).astype(jnp.bfloat16)

def adapter_terms(active_rows, key_value_cotangent, adapter_down, adapter_up):
    key_cotangent_rows = key_value_cotangent[:, :KEY_HEAD_WIDTH]
    value_cotangent_rows = key_value_cotangent[:, KEY_HEAD_WIDTH:]
    raise_key = jnp.dot(key_cotangent_rows, adapter_up[:ADAPTER_RANK].T, preferred_element_type=jnp.float32)
    raise_value = jnp.dot(value_cotangent_rows, adapter_up[ADAPTER_RANK:].T, preferred_element_type=jnp.float32)
    lift = jnp.concatenate([raise_key, raise_value], axis=1).astype(jnp.bfloat16)
    down_factor_grad = jnp.dot(active_rows.T, lift, preferred_element_type=jnp.float32)
    down_product = jnp.dot(active_rows, adapter_down, preferred_element_type=jnp.float32).astype(jnp.bfloat16)
    up_key = jnp.dot(key_cotangent_rows.T, down_product[:, :ADAPTER_RANK], preferred_element_type=jnp.float32)
    up_value = jnp.dot(value_cotangent_rows.T, down_product[:, ADAPTER_RANK:], preferred_element_type=jnp.float32)
    return (down_factor_grad, jnp.concatenate([up_key, up_value], axis=1))

def reference(activations, queries, rotated_key_value, attention_out_grad, adapter_down, adapter_up, bin_local_index, bin_row_offset, spill_node, spill_row_offset, arrival_pick_index, packed_sequence_number):
    entries = TOK_DEV + N_LOCAL * CAP_L + N_NODE * CAP_N
    device = jnp.broadcast_to(jnp.arange(BINS, dtype=jnp.int32)[:, None], (BINS, TOK_DEV))
    row_ids = jnp.broadcast_to(jnp.arange(TOK_DEV, dtype=jnp.int32)[None, :], (BINS, TOK_DEV))
    dev_node = device // N_LOCAL
    dev_local = device % N_LOCAL
    moved_in = bin_local_index != dev_local
    moved_out = spill_node != dev_node
    dest_device = jnp.where(moved_in, dev_node * N_LOCAL + bin_local_index, jnp.where(moved_out, spill_node * N_LOCAL + dev_local, device))
    dest_entry = jnp.where(moved_in, TOK_DEV + dev_local * CAP_L + bin_row_offset, jnp.where(moved_out, TOK_DEV + N_LOCAL * CAP_L + dev_node * CAP_N + spill_row_offset, row_ids))
    source_ids = (device * TOK_DEV + row_ids).astype(jnp.int32)
    flat_dest = (dest_device * entries + dest_entry).astype(jnp.int32).reshape(-1)
    source_table = jnp.zeros((BINS * entries,), jnp.int32).at[flat_dest].set(source_ids.reshape(-1))
    bin_ids = jnp.arange(BINS, dtype=jnp.int32)[:, None]
    picks = source_table[(bin_ids * entries + arrival_pick_index).astype(jnp.int32).reshape(-1)].reshape(BINS, TOK_DEV)

    def one_bin(running, bin_inputs):
        select_rows, segments = bin_inputs
        key_value_cotangent = bin_backward(queries[select_rows], rotated_key_value[select_rows], attention_out_grad[select_rows], segments)
        down_contribution, up_contribution = adapter_terms(activations[select_rows], key_value_cotangent, adapter_down, adapter_up)
        return ((running[0] + down_contribution, running[1] + up_contribution), key_value_cotangent)
    start_sums = (jnp.zeros((MODEL_WIDTH, 2 * ADAPTER_RANK), jnp.float32), jnp.zeros((KEY_HEAD_WIDTH, 2 * ADAPTER_RANK), jnp.float32))
    totals, kv_grads = lax.scan(one_bin, start_sums, (picks, packed_sequence_number))
    factor = 1.0 / jnp.sqrt(jnp.float32(BINS * TOK_DEV))
    return (kv_grads.reshape(BINS * TOK_DEV, 2 * KEY_HEAD_WIDTH), totals[0] * factor, totals[1] * factor)
```

```python
import functools
import math

import jax
import jax.numpy as jnp
import numpy as np
from jax import lax
from jax.experimental import pallas as pl
from jax.experimental.pallas import tpu as pltpu
from jax.sharding import PartitionSpec as P

KV_HEADS = 8
HEAD = 128
ADAPTER_RANK = 64
CAP = 4
GROUP = 5
KEY_HEAD_WIDTH = 1024
CHUNK = 16
GW = (2 * GROUP + 2) * HEAD
GQ = GW // 4
ROPE_THETA = 1000000.0
F32 = jnp.float32
BF16 = jnp.bfloat16


def dot(a, b):
    return jnp.dot(a, b, preferred_element_type=F32)


def dot_t(a, b):
    return lax.dot_general(a, b, (((1,), (1,)), ((), ())), preferred_element_type=F32)


def dot_l(a, b):
    return lax.dot_general(a, b, (((0,), (0,)), ((), ())), preferred_element_type=F32)


def iota(shape, axis):
    return lax.broadcasted_iota(jnp.int32, shape, axis)


def column(row):
    rows = row.shape[1]
    wide = jnp.broadcast_to(row.astype(F32), (128, rows))
    return jnp.transpose(wide)[:, 0:1].astype(jnp.int32)


def main_kernel(
    n_local,
    n_node,
    x_hbm,
    q_hbm,
    kv_hbm,
    g_hbm,
    down_hbm,
    up_ref,
    bl_ref,
    bo_ref,
    sn_ref,
    so_ref,
    pick_ref,
    seg_ref,
    cot_hbm,
    ddown_ref,
    dup_ref,
    stage,
    x_st,
    down_v,
    send,
    send_x,
    arr,
    arr_x,
    pack_hot,
    own_hot,
    arr_hot,
    bias,
    cos_v,
    sin_v,
    pk,
    xp,
    keys_out,
    vals_out,
    lift,
    load_sem,
    xload_sem,
    out_sem,
    send_sem,
    recv_sem,
):
    rows = x_st.shape[0]
    width = x_st.shape[1]
    xq = width // 4
    own_l = lax.axis_index("local")
    own_n = lax.axis_index("node")
    peers = n_local + n_node
    entries = peers * CHUNK

    def load(j):
        copies = []
        spans = (
            (q_hbm, j * (GROUP * HEAD), GROUP * HEAD, 0),
            (g_hbm, j * (GROUP * HEAD), GROUP * HEAD, GROUP * HEAD),
            (kv_hbm, j * HEAD, HEAD, 2 * GROUP * HEAD),
            (kv_hbm, KEY_HEAD_WIDTH + j * HEAD, HEAD, (2 * GROUP + 1) * HEAD),
        )
        for i, (src, at, size, to) in enumerate(spans):
            copies.append(
                pltpu.make_async_copy(
                    src.at[:, pl.ds(pl.multiple_of(at, HEAD), size)],
                    stage.at[j, :, to : to + size],
                    load_sem.at[j, i],
                )
            )
        return copies

    x_copy = pltpu.make_async_copy(x_hbm, x_st, xload_sem.at[0])
    down_copy = pltpu.make_async_copy(down_hbm, down_v, xload_sem.at[1])

    barrier = pltpu.get_barrier_semaphore()
    for o in range(1, n_local):
        pl.semaphore_signal(
            barrier,
            inc=1,
            device_id={"local": lax.rem(own_l + o, n_local)},
            device_id_type=pl.DeviceIdType.MESH,
        )
    for o in range(1, n_node):
        pl.semaphore_signal(
            barrier,
            inc=1,
            device_id={"node": lax.rem(own_n + o, n_node)},
            device_id_type=pl.DeviceIdType.MESH,
        )

    def start_load(j, c):
        for copy in load(j):
            copy.start()
        return c

    lax.fori_loop(0, KV_HEADS, start_load, 0)
    x_copy.start()
    down_copy.start()

    moved_in = bl_ref[...] != own_l
    moved_out = sn_ref[...] != own_n
    code = jnp.where(
        moved_in,
        bl_ref[...] * CAP + bo_ref[...],
        jnp.where(moved_out, (n_local + sn_ref[...]) * CAP + so_ref[...], -1),
    )
    a_sub = iota((entries, rows), 0)
    hit = code == (a_sub // CHUNK) * CAP + a_sub % CAP
    for c in range(4):
        pack_hot[c] = jnp.where(hit & ((a_sub // CAP) % 4 == c), 1.0, 0.0).astype(BF16)
    pick = column(pick_ref[...])
    own_hot[...] = jnp.where(pick == iota((rows, rows), 1), 1.0, 0.0).astype(BF16)
    a_lane = iota((rows, entries), 1)
    got = pick == rows + (a_lane // CHUNK) * CAP + a_lane % CAP
    for c in range(4):
        arr_hot[c] = jnp.where(got & ((a_lane // CAP) % 4 == c), 1.0, 0.0).astype(BF16)

    for slot in (own_l, n_local + own_n):
        arr_x[slot] = jnp.zeros(arr_x.shape[1:], BF16)

    def clear(j, c):
        for slot in (own_l, n_local + own_n):
            arr[j, slot] = jnp.zeros(arr.shape[2:], BF16)
        return c

    lax.fori_loop(0, KV_HEADS, clear, 0)

    pl.semaphore_wait(barrier, n_local - 1 + n_node - 1)

    def message(j, axis, o, src, dst):
        count, me, base = (n_local, own_l, 0) if axis == "local" else (n_node, own_n, n_local)
        to = lax.rem(me + o, count)
        return pltpu.make_async_remote_copy(
            src_ref=src.at[base + to],
            dst_ref=dst.at[base + me],
            send_sem=send_sem.at[j, base + to],
            recv_sem=recv_sem.at[j, base + me],
            device_id={axis: to},
            device_id_type=pl.DeviceIdType.MESH,
        )

    def arrival(j, axis, o, src, dst):
        count, me, base = (n_local, own_l, 0) if axis == "local" else (n_node, own_n, n_local)
        frm = lax.rem(me + count - o, count)
        return pltpu.make_async_remote_copy(
            src_ref=src.at[base + frm],
            dst_ref=dst.at[base + frm],
            send_sem=send_sem.at[j, base + frm],
            recv_sem=recv_sem.at[j, base + frm],
            device_id={axis: frm},
            device_id_type=pl.DeviceIdType.MESH,
        )

    hops = [("node", o) for o in range(1, n_node)] + [("local", o) for o in range(1, n_local)]

    def pack(j, carry):
        for copy in load(j):
            copy.wait()
        total = dot(pack_hot[0], stage[j, :, 0:GQ])
        for c in range(1, 4):
            total += dot(pack_hot[c], stage[j, :, c * GQ : (c + 1) * GQ])
        send[j] = total.astype(BF16).reshape(peers, CHUNK, GQ)
        for axis, o in hops:
            message(j, axis, o, send.at[j], arr.at[j]).start()
        return carry

    lax.fori_loop(0, KV_HEADS, pack, 0)
    x_copy.wait()
    total = dot(pack_hot[0], x_st[:, 0:xq])
    for c in range(1, 4):
        total += dot(pack_hot[c], x_st[:, c * xq : (c + 1) * xq])
    send_x[...] = total.astype(BF16).reshape(peers, CHUNK, xq)
    for axis, o in hops:
        message(KV_HEADS, axis, o, send_x, arr_x).start()

    seg_row = seg_ref[...]
    seg_col = column(seg_row)
    allowed = (seg_col == seg_row) & (iota((rows, rows), 0) <= iota((rows, rows), 1))
    bias[...] = jnp.where(allowed, 0.0, -1e30)
    first = jnp.sum(jnp.where(seg_row < seg_col, 1.0, 0.0), axis=1, keepdims=True)
    position = iota((rows, HEAD), 0).astype(F32) - first
    lane = iota((rows, HEAD), 1)
    half = lane % (HEAD // 2)
    frequency = jnp.exp(half.astype(F32) * (-2.0 * math.log(ROPE_THETA) / HEAD))
    angles = position * frequency
    cos_v[...] = jnp.cos(angles)
    sin_v[...] = jnp.where(lane < HEAD // 2, jnp.sin(angles), -jnp.sin(angles))
    lift[...] = jnp.zeros_like(lift)

    scale = 1.0 / math.sqrt(HEAD)
    exp_scale = scale * math.log2(math.e)
    up_row = iota((2 * ADAPTER_RANK, HEAD), 0)

    def cot_copies(j):
        return (
            pltpu.make_async_copy(
                keys_out.at[j],
                cot_hbm.at[:, pl.ds(pl.multiple_of(j * HEAD, HEAD), HEAD)],
                out_sem.at[j, 0],
            ),
            pltpu.make_async_copy(
                vals_out.at[j],
                cot_hbm.at[:, pl.ds(pl.multiple_of(KEY_HEAD_WIDTH + j * HEAD, HEAD), HEAD)],
                out_sem.at[j, 1],
            ),
        )

    def head(j, carry):
        for axis, o in hops:
            arrival(j, axis, o, send.at[j], arr.at[j]).wait_recv()
        arrived = arr[j].reshape(entries, GQ)
        for c in range(4):
            part = dot(own_hot[...], stage[j, :, c * GQ : (c + 1) * GQ])
            part += dot(arr_hot[c], arrived)
            pk[:, c * GQ : (c + 1) * GQ] = part.astype(BF16)
        k = pk[:, 2 * GROUP * HEAD : (2 * GROUP + 1) * HEAD]
        v = pk[:, (2 * GROUP + 1) * HEAD :]
        d_key = jnp.zeros((rows, HEAD), F32)
        d_val = jnp.zeros((rows, HEAD), F32)
        for h in range(GROUP):
            q = pk[:, h * HEAD : (h + 1) * HEAD]
            g = pk[:, (GROUP + h) * HEAD : (GROUP + h + 1) * HEAD]
            scores = dot_t(k, q) + bias[...]
            top = jnp.max(scores, axis=0, keepdims=True)
            weights = jnp.exp2((scores - top) * exp_scale)
            probs = weights * (1.0 / jnp.sum(weights, axis=0, keepdims=True))
            prob_grad = dot_t(v, g)
            delta = jnp.sum(probs * prob_grad, axis=0, keepdims=True)
            score_grad = (probs * (prob_grad - delta)).astype(BF16)
            d_val += dot(probs.astype(BF16), g)
            d_key += dot(score_grad, q)
        d_key = d_key * scale
        d_key = d_key * cos_v[...] + pltpu.roll(d_key, HEAD // 2, 1) * sin_v[...]
        key_low = d_key.astype(BF16)
        val_low = d_val.astype(BF16)
        keys_out[j] = key_low
        vals_out[j] = val_low
        for copy in cot_copies(j):
            copy.start()
        up = up_ref[:, pl.ds(pl.multiple_of(j * HEAD, HEAD), HEAD)].astype(F32)
        up_key = jnp.where(up_row < ADAPTER_RANK, up, 0.0).astype(BF16)
        up_val = jnp.where(up_row < ADAPTER_RANK, 0.0, up).astype(BF16)
        lift[...] += dot_t(key_low, up_key) + dot_t(val_low, up_val)
        return carry

    lax.fori_loop(0, KV_HEADS, head, 0)

    for axis, o in hops:
        arrival(KV_HEADS, axis, o, send_x, arr_x).wait_recv()
    arrived = arr_x[...].reshape(entries, xq)
    down_copy.wait()
    down_out = jnp.zeros((rows, 2 * ADAPTER_RANK), F32)
    lift_low = lift[...].astype(BF16)
    for c in range(4):
        part = dot(own_hot[...], x_st[:, c * xq : (c + 1) * xq])
        part += dot(arr_hot[c], arrived)
        part = part.astype(BF16)
        xp[...] = part
        down_out += dot(part, down_v[c * xq : (c + 1) * xq, :])
        ddown_ref[c * xq : (c + 1) * xq, :] = dot_l(xp[...], lift_low)
    down_low = down_out.astype(BF16)
    down_lane = iota((HEAD, 2 * ADAPTER_RANK), 1) < ADAPTER_RANK

    def up_grad(j, carry):
        from_key = dot_l(keys_out[j], down_low)
        from_val = dot_l(vals_out[j], down_low)
        dup_ref[pl.ds(pl.multiple_of(j * HEAD, HEAD), HEAD), :] = jnp.where(
            down_lane, from_key, from_val
        )
        return carry

    lax.fori_loop(0, KV_HEADS, up_grad, 0)

    def finish(j, carry):
        for copy in cot_copies(j):
            copy.wait()
        for axis, o in hops:
            message(j, axis, o, send.at[j], arr.at[j]).wait_send()
        return carry

    lax.fori_loop(0, KV_HEADS, finish, 0)
    for axis, o in hops:
        message(KV_HEADS, axis, o, send_x, arr_x).wait_send()


def sum_kernel(
    n_local,
    n_node,
    factor,
    a_ref,
    b_ref,
    a_out,
    b_out,
    send_a,
    recv_a,
    send_b,
    recv_b,
    send_c,
    recv_c,
    mid,
    last,
    sem_a,
    sem_b,
    sem_c,
):
    n_x, n_z = n_local // 2, n_node // 2
    own_l = lax.axis_index("local")
    own_n = lax.axis_index("node")
    core, lx = lax.rem(own_l, 2), own_l // 2
    y, z = lax.rem(own_n, 2), own_n // 2
    a_rows = a_ref.shape[4]
    n_group = 2 * n_x
    own_g = y * n_x + lx
    mesh_id = pl.DeviceIdType.MESH

    sibling = {"local": lx * 2 + (1 - core), "node": own_n}
    group = []
    for o in range(1, n_group):
        g = lax.rem(own_g + o, n_group)
        group.append((g, {"local": lax.rem(g, n_x) * 2 + core, "node": z * 2 + g // n_x}))
    far = []
    for o in range(1, n_z):
        t = lax.rem(z + o, n_z)
        far.append((t, {"local": own_l, "node": t * 2 + y}))

    barrier = pltpu.get_barrier_semaphore()
    targets = [sibling] + [d for _, d in group] + [d for _, d in far]
    for d in targets:
        pl.semaphore_signal(barrier, inc=1, device_id=d, device_id_type=mesh_id)

    for yy in range(2):
        for xx in range(n_x):
            g = yy * n_x + xx
            send_a[g, :, :a_rows, :] = a_ref[:, yy, xx, 1 - core].astype(BF16)
            send_a[g, :, a_rows:, :] = b_ref[:, yy, xx, 1 - core].astype(BF16)
    pl.semaphore_wait(barrier, len(targets))
    copies_a = []
    for o in range(n_group):
        g = lax.rem(own_g + 1 + o, n_group)
        copy = pltpu.make_async_remote_copy(
            src_ref=send_a.at[g],
            dst_ref=recv_a.at[g],
            send_sem=sem_a.at[0, g],
            recv_sem=sem_a.at[1, g],
            device_id=sibling,
            device_id_type=mesh_id,
        )
        copy.start()
        copies_a.append((g, copy))

    copies_b = []
    for o in range(n_group):
        g, copy = copies_a[o]
        copy.wait_recv()
        yy, xx = g // n_x, lax.rem(g, n_x)
        top = a_ref[:, yy, xx, core] + recv_a[g, :, :a_rows, :].astype(F32)
        low = b_ref[:, yy, xx, core] + recv_a[g, :, a_rows:, :].astype(F32)
        if o < n_group - 1:
            send_b[g, :, :a_rows, :] = top.astype(BF16)
            send_b[g, :, a_rows:, :] = low.astype(BF16)
            out = pltpu.make_async_remote_copy(
                src_ref=send_b.at[g],
                dst_ref=recv_b.at[own_g],
                send_sem=sem_b.at[0, g],
                recv_sem=sem_b.at[1, own_g],
                device_id=group[o][1],
                device_id_type=mesh_id,
            )
            out.start()
            copies_b.append(out)
        else:
            mid[:, :a_rows, :] = top
            mid[:, a_rows:, :] = low

    for g, d in group:
        pltpu.make_async_remote_copy(
            src_ref=send_b.at[g],
            dst_ref=recv_b.at[g],
            send_sem=sem_b.at[0, g],
            recv_sem=sem_b.at[1, g],
            device_id=d,
            device_id_type=mesh_id,
        ).wait_recv()
        mid[...] += recv_b[g].astype(F32)

    copies_c = []
    for t, d in far:
        send_c[t] = mid[t].astype(BF16)
        out = pltpu.make_async_remote_copy(
            src_ref=send_c.at[t],
            dst_ref=recv_c.at[z],
            send_sem=sem_c.at[0, t],
            recv_sem=sem_c.at[1, z],
            device_id=d,
            device_id_type=mesh_id,
        )
        out.start()
        copies_c.append(out)
    last[...] = mid[z]
    for t, d in far:
        pltpu.make_async_remote_copy(
            src_ref=send_c.at[t],
            dst_ref=recv_c.at[t],
            send_sem=sem_c.at[0, t],
            recv_sem=sem_c.at[1, t],
            device_id=d,
            device_id_type=mesh_id,
        ).wait_recv()
        last[...] += recv_c[t].astype(F32)
    a_out[...] = last[:a_rows, :] * factor
    b_out[...] = last[a_rows:, :] * factor
    for _, copy in copies_a:
        copy.wait_send()
    for copy in copies_b + copies_c:
        copy.wait_send()


def factor_sums(n_local, n_node, factor, a, b):
    n_x, n_z = n_local // 2, n_node // 2
    n_dev = n_local * n_node

    def lay(v):
        size = v.shape[0] // n_dev
        padded = -(-size // 16) * 16
        v = v.reshape(n_dev, size, v.shape[1])
        if padded != size:
            v = jnp.pad(v, ((0, 0), (0, padded - size), (0, 0)))
        return v.reshape(n_z, 2, n_x, 2, padded, v.shape[2]), size, padded

    a, a_size, a_rows = lay(a)
    b, b_size, b_rows = lay(b)
    rows = a_rows + b_rows
    wide = a.shape[-1]
    n_group = 2 * n_x
    vmem = pl.BlockSpec(memory_space=pltpu.VMEM)
    a_out, b_out = pl.pallas_call(
        functools.partial(sum_kernel, n_local, n_node, factor),
        out_shape=(
            jax.ShapeDtypeStruct((a_rows, wide), F32),
            jax.ShapeDtypeStruct((b_rows, wide), F32),
        ),
        in_specs=[vmem, vmem],
        out_specs=(vmem, vmem),
        scratch_shapes=[
            pltpu.VMEM((n_group, n_z, rows, wide), BF16),
            pltpu.VMEM((n_group, n_z, rows, wide), BF16),
            pltpu.VMEM((n_group, n_z, rows, wide), BF16),
            pltpu.VMEM((n_group, n_z, rows, wide), BF16),
            pltpu.VMEM((n_z, rows, wide), BF16),
            pltpu.VMEM((n_z, rows, wide), BF16),
            pltpu.VMEM((n_z, rows, wide), F32),
            pltpu.VMEM((rows, wide), F32),
            pltpu.SemaphoreType.DMA((2, n_group)),
            pltpu.SemaphoreType.DMA((2, n_group)),
            pltpu.SemaphoreType.DMA((2, n_z)),
        ],
        compiler_params=pltpu.CompilerParams(
            collective_id=1, has_side_effects=True, vmem_limit_bytes=48 * 2**20
        ),
        name="factor_sums",
    )(a, b)
    return a_out[:a_size], b_out[:b_size]


def local(n_local, n_node, *args):
    activations, queries, rotated_key_value, attention_out_grad, adapter_down, adapter_up = args[:6]
    rows, width = activations.shape
    peers = n_local + n_node
    entries = peers * CHUNK
    vmem = pl.BlockSpec(memory_space=pltpu.VMEM)
    hbm = pl.BlockSpec(memory_space=pl.ANY)
    cotangent, down_grad, up_grad = pl.pallas_call(
        functools.partial(main_kernel, n_local, n_node),
        out_shape=(
            jax.ShapeDtypeStruct((rows, 2 * KEY_HEAD_WIDTH), BF16),
            jax.ShapeDtypeStruct((width, 2 * ADAPTER_RANK), F32),
            jax.ShapeDtypeStruct((KEY_HEAD_WIDTH, 2 * ADAPTER_RANK), F32),
        ),
        in_specs=[hbm] * 5 + [vmem] * 7,
        out_specs=(hbm, vmem, vmem),
        scratch_shapes=[
            pltpu.VMEM((KV_HEADS, rows, GW), BF16),
            pltpu.VMEM((rows, width), BF16),
            pltpu.VMEM((width, 2 * ADAPTER_RANK), BF16),
            pltpu.VMEM((KV_HEADS, peers, CHUNK, GQ), BF16),
            pltpu.VMEM((peers, CHUNK, width // 4), BF16),
            pltpu.VMEM((KV_HEADS, peers, CHUNK, GQ), BF16),
            pltpu.VMEM((peers, CHUNK, width // 4), BF16),
            pltpu.VMEM((4, entries, rows), BF16),
            pltpu.VMEM((rows, rows), BF16),
            pltpu.VMEM((4, rows, entries), BF16),
            pltpu.VMEM((rows, rows), F32),
            pltpu.VMEM((rows, HEAD), F32),
            pltpu.VMEM((rows, HEAD), F32),
            pltpu.VMEM((rows, GW), BF16),
            pltpu.VMEM((rows, width // 4), BF16),
            pltpu.VMEM((KV_HEADS, rows, HEAD), BF16),
            pltpu.VMEM((KV_HEADS, rows, HEAD), BF16),
            pltpu.VMEM((rows, 2 * ADAPTER_RANK), F32),
            pltpu.SemaphoreType.DMA((KV_HEADS, 4)),
            pltpu.SemaphoreType.DMA((2,)),
            pltpu.SemaphoreType.DMA((KV_HEADS, 2)),
            pltpu.SemaphoreType.DMA((KV_HEADS + 1, peers)),
            pltpu.SemaphoreType.DMA((KV_HEADS + 1, peers)),
        ],
        compiler_params=pltpu.CompilerParams(
            collective_id=0, has_side_effects=True, vmem_limit_bytes=48 * 2**20
        ),
        name="exchange_attention",
    )(*args)
    factor = 1.0 / math.sqrt(rows * n_local * n_node)
    down_sum, up_sum = factor_sums(n_local, n_node, factor, down_grad, up_grad)
    return cotangent, down_sum, up_sum


def solution(mesh):
    placed = (P(("node", "local"), None),) * 4 + (P(),) * 2 + (P(("node", "local"), None),) * 6
    return jax.shard_map(
        functools.partial(local, mesh.shape["local"], mesh.shape["node"]),
        mesh=mesh,
        in_specs=placed,
        out_specs=(P(("node", "local"), None),) * 3,
        check_vma=False,
    )
```

```python
import functools
import math

import jax
import jax.numpy as jnp
import numpy as np
from jax import lax
from jax.experimental import pallas as pl
from jax.experimental.pallas import tpu as pltpu
from jax.sharding import PartitionSpec as P

KV_HEADS = 8
HEAD = 128
ADAPTER_RANK = 64
CAP = 4
GROUP = 5
KEY_HEAD_WIDTH = 1024
CHUNK = 16
GW = (2 * GROUP + 2) * HEAD
GQ = GW // 4
ROPE_THETA = 1000000.0
F32 = jnp.float32
BF16 = jnp.bfloat16


def dot(a, b):
    return jnp.dot(a, b, preferred_element_type=F32)


def dot_t(a, b):
    return lax.dot_general(a, b, (((1,), (1,)), ((), ())), preferred_element_type=F32)


def dot_l(a, b):
    return lax.dot_general(a, b, (((0,), (0,)), ((), ())), preferred_element_type=F32)


def iota(shape, axis):
    return lax.broadcasted_iota(jnp.int32, shape, axis)


def column(row):
    rows = row.shape[1]
    wide = jnp.broadcast_to(row.astype(F32), (128, rows))
    return jnp.transpose(wide)[:, 0:1].astype(jnp.int32)


def main_kernel(
    n_local,
    n_node,
    x_hbm,
    q_hbm,
    kv_hbm,
    g_hbm,
    down_hbm,
    up_hbm,
    bl_hbm,
    bo_hbm,
    sn_hbm,
    so_hbm,
    pick_hbm,
    seg_hbm,
    cot_hbm,
    ddown_ref,
    dup_ref,
    ints,
    up_ref,
    stage,
    x_st,
    x_turned,
    down_v,
    down_rows,
    send,
    send_d,
    send_l,
    arr,
    arr_d,
    arr_l,
    pack_hot,
    own_hot,
    arr_hot,
    bias,
    cos_v,
    sin_v,
    qs,
    gs,
    kvs,
    probs_s,
    grads_s,
    keys_out,
    vals_out,
    lift,
    int_sem,
    load_sem,
    xload_sem,
    out_sem,
    send_sem,
    recv_sem,
):
    rows = x_st.shape[0]
    width = x_st.shape[1]
    block = HEAD
    own_l = lax.axis_index("local")
    own_n = lax.axis_index("node")
    peers = n_local + n_node
    entries = peers * CHUNK

    def load(j):
        copies = []
        spans = (
            (q_hbm, j * (GROUP * HEAD), GROUP * HEAD, 0),
            (g_hbm, j * (GROUP * HEAD), GROUP * HEAD, GROUP * HEAD),
            (kv_hbm, j * HEAD, HEAD, 2 * GROUP * HEAD),
            (kv_hbm, KEY_HEAD_WIDTH + j * HEAD, HEAD, (2 * GROUP + 1) * HEAD),
        )
        for i, (src, at, size, to) in enumerate(spans):
            copies.append(
                pltpu.make_async_copy(
                    src.at[:, pl.ds(pl.multiple_of(at, HEAD), size)],
                    stage.at[j, :, to : to + size],
                    load_sem.at[j, i],
                )
            )
        return copies

    x_copy = pltpu.make_async_copy(x_hbm, x_st, xload_sem.at[0])
    down_copy = pltpu.make_async_copy(down_hbm, down_v, xload_sem.at[1])
    up_copy = pltpu.make_async_copy(up_hbm, up_ref, xload_sem.at[2])
    int_copies = [
        pltpu.make_async_copy(src, ints.at[i], int_sem.at[i])
        for i, src in enumerate((bl_hbm, bo_hbm, sn_hbm, so_hbm, pick_hbm, seg_hbm))
    ]
    for copy in int_copies:
        copy.start()

    barrier = pltpu.get_barrier_semaphore()
    for o in range(1, n_local):
        pl.semaphore_signal(
            barrier,
            inc=1,
            device_id={"local": lax.rem(own_l + o, n_local)},
            device_id_type=pl.DeviceIdType.MESH,
        )
    for o in range(1, n_node):
        pl.semaphore_signal(
            barrier,
            inc=1,
            device_id={"node": lax.rem(own_n + o, n_node)},
            device_id_type=pl.DeviceIdType.MESH,
        )

    def start_load(j, c):
        for copy in load(j):
            copy.start()
        return c

    lax.fori_loop(0, KV_HEADS, start_load, 0)
    x_copy.start()
    down_copy.start()
    up_copy.start()
    for copy in int_copies:
        copy.wait()
    near_bin, near_off, far_bin, far_off = ints[0], ints[1], ints[2], ints[3]

    moved_in = near_bin != own_l
    moved_out = far_bin != own_n
    code = jnp.where(
        moved_in,
        near_bin * CAP + near_off,
        jnp.where(moved_out, (n_local + far_bin) * CAP + far_off, -1),
    )
    a_sub = iota((entries, rows), 0)
    hit = code == (a_sub // CHUNK) * CAP + a_sub % CAP
    for c in range(4):
        pack_hot[c] = jnp.where(hit & ((a_sub // CAP) % 4 == c), 1.0, 0.0).astype(BF16)
    pick = column(ints[4])
    own_hot[...] = jnp.where(pick == iota((rows, rows), 1), 1.0, 0.0).astype(BF16)
    a_lane = iota((rows, entries), 1)
    got = pick == rows + (a_lane // CHUNK) * CAP + a_lane % CAP
    for c in range(4):
        arr_hot[c] = jnp.where(got & ((a_lane // CAP) % 4 == c), 1.0, 0.0).astype(BF16)

    for slot in (own_l, n_local + own_n):
        arr_d[slot] = jnp.zeros(arr_d.shape[1:], BF16)
        arr_l[slot] = jnp.zeros(arr_l.shape[1:], BF16)

    def clear(j, c):
        for slot in (own_l, n_local + own_n):
            arr[j, slot] = jnp.zeros(arr.shape[2:], BF16)
        return c

    lax.fori_loop(0, KV_HEADS, clear, 0)

    pl.semaphore_wait(barrier, n_local - 1 + n_node - 1)

    def message(j, axis, o, src, dst):
        count, me, base = (n_local, own_l, 0) if axis == "local" else (n_node, own_n, n_local)
        to = lax.rem(me + o, count)
        return pltpu.make_async_remote_copy(
            src_ref=src.at[base + to],
            dst_ref=dst.at[base + me],
            send_sem=send_sem.at[j, base + to],
            recv_sem=recv_sem.at[j, base + me],
            device_id={axis: to},
            device_id_type=pl.DeviceIdType.MESH,
        )

    def arrival(j, axis, o, src, dst):
        count, me, base = (n_local, own_l, 0) if axis == "local" else (n_node, own_n, n_local)
        frm = lax.rem(me + count - o, count)
        return pltpu.make_async_remote_copy(
            src_ref=src.at[base + frm],
            dst_ref=dst.at[base + frm],
            send_sem=send_sem.at[j, base + frm],
            recv_sem=recv_sem.at[j, base + frm],
            device_id={axis: frm},
            device_id_type=pl.DeviceIdType.MESH,
        )

    hops = [("node", o) for o in range(1, n_node)] + [("local", o) for o in range(1, n_local)]

    def pack(j, carry):
        for copy in load(j):
            copy.wait()
        total = dot(pack_hot[0], stage[j, :, 0:GQ])
        for c in range(1, 4):
            total += dot(pack_hot[c], stage[j, :, c * GQ : (c + 1) * GQ])
        send[j] = total.astype(BF16).reshape(peers, CHUNK, GQ)
        for axis, o in hops:
            message(j, axis, o, send.at[j], arr.at[j]).start()
        return carry

    lax.fori_loop(0, KV_HEADS, pack, 0)
    x_copy.wait()
    down_copy.wait()
    down_rows[...] = dot(x_st[...], down_v[...]).astype(BF16)
    send_d[...] = dot(pack_hot[0], down_rows[...]).astype(BF16).reshape(send_d.shape)
    for axis, o in hops:
        message(KV_HEADS, axis, o, send_d, arr_d).start()

    seg_row = ints[5]
    seg_col = column(seg_row)
    allowed = (seg_col == seg_row) & (iota((rows, rows), 0) <= iota((rows, rows), 1))
    bias[...] = jnp.where(allowed, 0.0, -1e30)
    first = jnp.sum(jnp.where(seg_row < seg_col, 1.0, 0.0), axis=1, keepdims=True)
    position = iota((rows, HEAD), 0).astype(F32) - first
    lane = iota((rows, HEAD), 1)
    half = lane % (HEAD // 2)
    frequency = jnp.exp(half.astype(F32) * (-2.0 * math.log(ROPE_THETA) / HEAD))
    angles = position * frequency
    cos_v[...] = jnp.cos(angles)
    sin_v[...] = jnp.where(lane < HEAD // 2, jnp.sin(angles), -jnp.sin(angles))
    lift[...] = jnp.zeros_like(lift)

    def turn(i, carry):
        at = pl.multiple_of(i * HEAD, HEAD)
        x_turned[pl.ds(at, HEAD), :] = jnp.transpose(x_st[:, pl.ds(at, HEAD)])
        return carry

    lax.fori_loop(0, width // HEAD, turn, 0)
    up_copy.wait()

    scale = 1.0 / math.sqrt(HEAD)
    exp_scale = scale * math.log2(math.e)
    up_row = iota((2 * ADAPTER_RANK, HEAD), 0)

    def cot_copies(j):
        return (
            pltpu.make_async_copy(
                keys_out.at[j],
                cot_hbm.at[:, pl.ds(pl.multiple_of(j * HEAD, HEAD), HEAD)],
                out_sem.at[j, 0],
            ),
            pltpu.make_async_copy(
                vals_out.at[j],
                cot_hbm.at[:, pl.ds(pl.multiple_of(KEY_HEAD_WIDTH + j * HEAD, HEAD), HEAD)],
                out_sem.at[j, 1],
            ),
        )

    def head(j, carry):
        for axis, o in hops:
            arrival(j, axis, o, send.at[j], arr.at[j]).wait_recv()
        arrived = arr[j].reshape(entries, GQ)
        for c in range(4):
            part = dot(own_hot[...], stage[j, :, c * GQ : (c + 1) * GQ])
            part += dot(arr_hot[c], arrived)
            part = part.astype(BF16)
            for i in range(3):
                col = c * 3 + i
                piece = part[:, i * HEAD : (i + 1) * HEAD]
                if col >= 2 * GROUP:
                    kvs[col - 2 * GROUP] = piece
                    continue
                dst, h = (qs, col) if col < GROUP else (gs, col - GROUP)
                for b in range(rows // block):
                    dst[b, h * block : (h + 1) * block, :] = piece[b * block : (b + 1) * block]
        d_keys = [jnp.zeros((block, HEAD), F32)] * (rows // block)
        d_vals = [jnp.zeros((block, HEAD), F32)] * (rows // block)
        for b in range(rows // block):
            seen = (b + 1) * block
            scores = dot_t(kvs[0, :seen, :], qs[b])
            prob_grads = dot_t(kvs[1, :seen, :], gs[b])
            mask = bias[:seen, b * block : (b + 1) * block]
            for h in range(GROUP):
                cols = slice(h * block, (h + 1) * block)
                score = scores[:, cols] + mask
                top = jnp.max(score, axis=0, keepdims=True)
                weights = jnp.exp2((score - top) * exp_scale)
                probs = weights * (1.0 / jnp.sum(weights, axis=0, keepdims=True))
                prob_grad = prob_grads[:, cols]
                delta = jnp.sum(probs * prob_grad, axis=0, keepdims=True)
                probs_s[b, :seen, cols] = probs.astype(BF16)
                grads_s[b, :seen, cols] = (probs * (prob_grad - delta)).astype(BF16)
            d_val = dot(probs_s[b, :seen, :], gs[b])
            d_key = dot(grads_s[b, :seen, :], qs[b])
            for t in range(b + 1):
                d_vals[t] += d_val[t * block : (t + 1) * block]
                d_keys[t] += d_key[t * block : (t + 1) * block]
        d_key = jnp.concatenate(d_keys, axis=0)
        d_val = jnp.concatenate(d_vals, axis=0)
        d_key = d_key * scale
        d_key = d_key * cos_v[...] + pltpu.roll(d_key, HEAD // 2, 1) * sin_v[...]
        key_low = d_key.astype(BF16)
        val_low = d_val.astype(BF16)
        keys_out[j] = key_low
        vals_out[j] = val_low
        for copy in cot_copies(j):
            copy.start()
        up = up_ref[:, pl.ds(pl.multiple_of(j * HEAD, HEAD), HEAD)].astype(F32)
        up_key = jnp.where(up_row < ADAPTER_RANK, up, 0.0).astype(BF16)
        up_val = jnp.where(up_row < ADAPTER_RANK, 0.0, up).astype(BF16)
        lift[...] += dot_t(key_low, up_key) + dot_t(val_low, up_val)
        return carry

    lax.fori_loop(0, KV_HEADS, head, 0)

    lift_low = lift[...].astype(BF16)
    send_l[...] = dot_l(arr_hot[0], lift_low).astype(BF16).reshape(send_l.shape)
    for axis, o in hops:
        message(KV_HEADS + 1, axis, o, send_l, arr_l).start()

    for axis, o in hops:
        arrival(KV_HEADS, axis, o, send_d, arr_d).wait_recv()
    down_out = dot(own_hot[...], down_rows[...])
    down_out += dot(arr_hot[0], arr_d[...].reshape(entries, HEAD))
    down_low = down_out.astype(BF16)
    down_lane = iota((HEAD, 2 * ADAPTER_RANK), 1) < ADAPTER_RANK

    def up_grad(j, carry):
        from_key = dot_l(keys_out[j], down_low)
        from_val = dot_l(vals_out[j], down_low)
        dup_ref[pl.ds(pl.multiple_of(j * HEAD, HEAD), HEAD), :] = jnp.where(
            down_lane, from_key, from_val
        )
        return carry

    lax.fori_loop(0, KV_HEADS, up_grad, 0)

    own_lift = dot_l(own_hot[...], lift_low)
    for axis, o in hops:
        arrival(KV_HEADS + 1, axis, o, send_l, arr_l).wait_recv()
    own_lift += dot_l(pack_hot[0], arr_l[...].reshape(entries, HEAD))
    own_lift = own_lift.astype(BF16)
    span = width // 8
    for c in range(8):
        ddown_ref[c * span : (c + 1) * span, :] = dot(
            x_turned[c * span : (c + 1) * span, :], own_lift
        )

    def finish(j, carry):
        for copy in cot_copies(j):
            copy.wait()
        for axis, o in hops:
            message(j, axis, o, send.at[j], arr.at[j]).wait_send()
        return carry

    lax.fori_loop(0, KV_HEADS, finish, 0)
    for axis, o in hops:
        message(KV_HEADS, axis, o, send_d, arr_d).wait_send()
        message(KV_HEADS + 1, axis, o, send_l, arr_l).wait_send()


def sum_kernel(
    n_local,
    n_node,
    factor,
    a_ref,
    b_ref,
    a_out,
    b_out,
    send_a,
    recv_a,
    send_b,
    recv_b,
    send_c,
    recv_c,
    mid,
    last,
    sem_a,
    sem_b,
    sem_c,
):
    n_x, n_z = n_local // 2, n_node // 2
    own_l = lax.axis_index("local")
    own_n = lax.axis_index("node")
    core, lx = lax.rem(own_l, 2), own_l // 2
    y, z = lax.rem(own_n, 2), own_n // 2
    a_rows = a_ref.shape[4]
    n_group = 2 * n_x
    own_g = y * n_x + lx
    mesh_id = pl.DeviceIdType.MESH

    sibling = {"local": lx * 2 + (1 - core), "node": own_n}
    group = []
    for o in range(1, n_group):
        g = lax.rem(own_g + o, n_group)
        group.append((g, {"local": lax.rem(g, n_x) * 2 + core, "node": z * 2 + g // n_x}))
    far = []
    for o in range(1, n_z):
        t = lax.rem(z + o, n_z)
        far.append((t, {"local": own_l, "node": t * 2 + y}))

    barrier = pltpu.get_barrier_semaphore()
    targets = [sibling] + [d for _, d in group] + [d for _, d in far]
    for d in targets:
        pl.semaphore_signal(barrier, inc=1, device_id=d, device_id_type=mesh_id)

    for yy in range(2):
        for xx in range(n_x):
            g = yy * n_x + xx
            send_a[g, :, :a_rows, :] = a_ref[:, yy, xx, 1 - core].astype(BF16)
            send_a[g, :, a_rows:, :] = b_ref[:, yy, xx, 1 - core].astype(BF16)
    pl.semaphore_wait(barrier, len(targets))
    copies_a = []
    for o in range(n_group):
        g = lax.rem(own_g + 1 + o, n_group)
        copy = pltpu.make_async_remote_copy(
            src_ref=send_a.at[g],
            dst_ref=recv_a.at[g],
            send_sem=sem_a.at[0, g],
            recv_sem=sem_a.at[1, g],
            device_id=sibling,
            device_id_type=mesh_id,
        )
        copy.start()
        copies_a.append((g, copy))

    copies_b = []
    for o in range(n_group):
        g, copy = copies_a[o]
        copy.wait_recv()
        yy, xx = g // n_x, lax.rem(g, n_x)
        top = a_ref[:, yy, xx, core] + recv_a[g, :, :a_rows, :].astype(F32)
        low = b_ref[:, yy, xx, core] + recv_a[g, :, a_rows:, :].astype(F32)
        if o < n_group - 1:
            send_b[g, :, :a_rows, :] = top.astype(BF16)
            send_b[g, :, a_rows:, :] = low.astype(BF16)
            out = pltpu.make_async_remote_copy(
                src_ref=send_b.at[g],
                dst_ref=recv_b.at[own_g],
                send_sem=sem_b.at[0, g],
                recv_sem=sem_b.at[1, own_g],
                device_id=group[o][1],
                device_id_type=mesh_id,
            )
            out.start()
            copies_b.append(out)
        else:
            mid[:, :a_rows, :] = top
            mid[:, a_rows:, :] = low

    for g, d in group:
        pltpu.make_async_remote_copy(
            src_ref=send_b.at[g],
            dst_ref=recv_b.at[g],
            send_sem=sem_b.at[0, g],
            recv_sem=sem_b.at[1, g],
            device_id=d,
            device_id_type=mesh_id,
        ).wait_recv()
        mid[...] += recv_b[g].astype(F32)

    copies_c = []
    for t, d in far:
        send_c[t] = mid[t].astype(BF16)
        out = pltpu.make_async_remote_copy(
            src_ref=send_c.at[t],
            dst_ref=recv_c.at[z],
            send_sem=sem_c.at[0, t],
            recv_sem=sem_c.at[1, z],
            device_id=d,
            device_id_type=mesh_id,
        )
        out.start()
        copies_c.append(out)
    last[...] = mid[z]
    for t, d in far:
        pltpu.make_async_remote_copy(
            src_ref=send_c.at[t],
            dst_ref=recv_c.at[t],
            send_sem=sem_c.at[0, t],
            recv_sem=sem_c.at[1, t],
            device_id=d,
            device_id_type=mesh_id,
        ).wait_recv()
        last[...] += recv_c[t].astype(F32)
    a_out[...] = last[:a_rows, :] * factor
    b_out[...] = last[a_rows:, :] * factor
    for _, copy in copies_a:
        copy.wait_send()
    for copy in copies_b + copies_c:
        copy.wait_send()


def factor_sums(n_local, n_node, factor, a, b):
    n_x, n_z = n_local // 2, n_node // 2
    n_dev = n_local * n_node

    def lay(v):
        size = v.shape[0] // n_dev
        padded = -(-size // 16) * 16
        v = v.reshape(n_dev, size, v.shape[1])
        if padded != size:
            v = jnp.pad(v, ((0, 0), (0, padded - size), (0, 0)))
        return v.reshape(n_z, 2, n_x, 2, padded, v.shape[2]), size, padded

    a, a_size, a_rows = lay(a)
    b, b_size, b_rows = lay(b)
    rows = a_rows + b_rows
    wide = a.shape[-1]
    n_group = 2 * n_x
    vmem = pl.BlockSpec(memory_space=pltpu.VMEM)
    a_out, b_out = pl.pallas_call(
        functools.partial(sum_kernel, n_local, n_node, factor),
        out_shape=(
            jax.ShapeDtypeStruct((a_rows, wide), F32),
            jax.ShapeDtypeStruct((b_rows, wide), F32),
        ),
        in_specs=[vmem, vmem],
        out_specs=(vmem, vmem),
        scratch_shapes=[
            pltpu.VMEM((n_group, n_z, rows, wide), BF16),
            pltpu.VMEM((n_group, n_z, rows, wide), BF16),
            pltpu.VMEM((n_group, n_z, rows, wide), BF16),
            pltpu.VMEM((n_group, n_z, rows, wide), BF16),
            pltpu.VMEM((n_z, rows, wide), BF16),
            pltpu.VMEM((n_z, rows, wide), BF16),
            pltpu.VMEM((n_z, rows, wide), F32),
            pltpu.VMEM((rows, wide), F32),
            pltpu.SemaphoreType.DMA((2, n_group)),
            pltpu.SemaphoreType.DMA((2, n_group)),
            pltpu.SemaphoreType.DMA((2, n_z)),
        ],
        compiler_params=pltpu.CompilerParams(
            collective_id=1, has_side_effects=True, vmem_limit_bytes=48 * 2**20
        ),
        name="factor_sums",
    )(a, b)
    return a_out[:a_size], b_out[:b_size]


def local(n_local, n_node, *args):
    activations, queries, rotated_key_value, attention_out_grad, adapter_down, adapter_up = args[:6]
    rows, width = activations.shape
    peers = n_local + n_node
    entries = peers * CHUNK
    vmem = pl.BlockSpec(memory_space=pltpu.VMEM)
    hbm = pl.BlockSpec(memory_space=pl.ANY)
    cotangent, down_grad, up_grad = pl.pallas_call(
        functools.partial(main_kernel, n_local, n_node),
        out_shape=(
            jax.ShapeDtypeStruct((rows, 2 * KEY_HEAD_WIDTH), BF16),
            jax.ShapeDtypeStruct((width, 2 * ADAPTER_RANK), F32),
            jax.ShapeDtypeStruct((KEY_HEAD_WIDTH, 2 * ADAPTER_RANK), F32),
        ),
        in_specs=[hbm] * 12,
        out_specs=(hbm, vmem, vmem),
        scratch_shapes=[
            pltpu.VMEM((6, 1, rows), jnp.int32),
            pltpu.VMEM(adapter_up.shape, BF16),
            pltpu.VMEM((KV_HEADS, rows, GW), BF16),
            pltpu.VMEM((rows, width), BF16),
            pltpu.VMEM((width, rows), BF16),
            pltpu.VMEM((width, 2 * ADAPTER_RANK), BF16),
            pltpu.VMEM((rows, 2 * ADAPTER_RANK), BF16),
            pltpu.VMEM((KV_HEADS, peers, CHUNK, GQ), BF16),
            pltpu.VMEM((peers, CHUNK, 2 * ADAPTER_RANK), BF16),
            pltpu.VMEM((peers, CHUNK, 2 * ADAPTER_RANK), BF16),
            pltpu.VMEM((KV_HEADS, peers, CHUNK, GQ), BF16),
            pltpu.VMEM((peers, CHUNK, 2 * ADAPTER_RANK), BF16),
            pltpu.VMEM((peers, CHUNK, 2 * ADAPTER_RANK), BF16),
            pltpu.VMEM((4, entries, rows), BF16),
            pltpu.VMEM((rows, rows), BF16),
            pltpu.VMEM((4, rows, entries), BF16),
            pltpu.VMEM((rows, rows), F32),
            pltpu.VMEM((rows, HEAD), F32),
            pltpu.VMEM((rows, HEAD), F32),
            pltpu.VMEM((rows // HEAD, GROUP * HEAD, HEAD), BF16),
            pltpu.VMEM((rows // HEAD, GROUP * HEAD, HEAD), BF16),
            pltpu.VMEM((2, rows, HEAD), BF16),
            pltpu.VMEM((rows // HEAD, rows, GROUP * HEAD), BF16),
            pltpu.VMEM((rows // HEAD, rows, GROUP * HEAD), BF16),
            pltpu.VMEM((KV_HEADS, rows, HEAD), BF16),
            pltpu.VMEM((KV_HEADS, rows, HEAD), BF16),
            pltpu.VMEM((rows, 2 * ADAPTER_RANK), F32),
            pltpu.SemaphoreType.DMA((6,)),
            pltpu.SemaphoreType.DMA((KV_HEADS, 4)),
            pltpu.SemaphoreType.DMA((3,)),
            pltpu.SemaphoreType.DMA((KV_HEADS, 2)),
            pltpu.SemaphoreType.DMA((KV_HEADS + 2, peers)),
            pltpu.SemaphoreType.DMA((KV_HEADS + 2, peers)),
        ],
        compiler_params=pltpu.CompilerParams(
            collective_id=0, has_side_effects=True, vmem_limit_bytes=48 * 2**20
        ),
        name="exchange_attention",
    )(*args)
    factor = 1.0 / math.sqrt(rows * n_local * n_node)
    down_sum, up_sum = factor_sums(n_local, n_node, factor, down_grad, up_grad)
    return cotangent, down_sum, up_sum


def solution(mesh):
    placed = (P(("node", "local"), None),) * 4 + (P(),) * 2 + (P(("node", "local"), None),) * 6
    return jax.shard_map(
        functools.partial(local, mesh.shape["local"], mesh.shape["node"]),
        mesh=mesh,
        in_specs=placed,
        out_specs=(P(("node", "local"), None),) * 3,
        check_vma=False,
    )
```

```python
import functools
import math

import jax
import jax.numpy as jnp
import numpy as np
from jax import lax
from jax.experimental import pallas as pl
from jax.experimental.pallas import tpu as pltpu
from jax.sharding import PartitionSpec as P

KV_HEADS = 8
HEAD = 128
ADAPTER_RANK = 64
CAP = 4
GROUP = 5
KEY_HEAD_WIDTH = 1024
CHUNK = 16
GW = (2 * GROUP + 2) * HEAD
PAIR = 2
ROUNDS = KV_HEADS // PAIR
GQ = PAIR * GW // 4
ROPE_THETA = 1000000.0
F32 = jnp.float32
BF16 = jnp.bfloat16


def dot(a, b):
    return jnp.dot(a, b, preferred_element_type=F32)


def dot_t(a, b):
    return lax.dot_general(a, b, (((1,), (1,)), ((), ())), preferred_element_type=F32)


def dot_l(a, b):
    return lax.dot_general(a, b, (((0,), (0,)), ((), ())), preferred_element_type=F32)


def iota(shape, axis):
    return lax.broadcasted_iota(jnp.int32, shape, axis)


def column(row):
    rows = row.shape[1]
    wide = jnp.broadcast_to(row.astype(F32), (128, rows))
    return jnp.transpose(wide)[:, 0:1].astype(jnp.int32)


def main_kernel(
    n_local,
    n_node,
    factor,
    x_hbm,
    q_hbm,
    kv_hbm,
    g_hbm,
    down_hbm,
    up_hbm,
    bl_hbm,
    bo_hbm,
    sn_hbm,
    so_hbm,
    pick_hbm,
    seg_hbm,
    cot_hbm,
    *rest,
):
    if factor is None:
        ddown_ref, dup_ref = rest[:2]
    else:
        down_sum, up_sum = rest[:2]
        dup_ref, send_a, recv_a, send_b, recv_b, send_c, recv_c = rest[-13:-6]
        own_part, mid, last, sem_a, sem_b, sem_c = rest[-6:]
    (
        ints,
        up_ref,
        stage,
        x_st,
        x_turned,
        down_v,
        down_rows,
        send,
        send_d,
        send_l,
        arr,
        arr_d,
        arr_l,
        pack_hot,
        own_hot,
        arr_hot,
        bias,
        cos_v,
        sin_v,
        qs,
        gs,
        kvs,
        probs_s,
        grads_s,
        keys_out,
        vals_out,
        lift,
        int_sem,
        load_sem,
        xload_sem,
        out_sem,
        send_sem,
        recv_sem,
    ) = rest[2:35]
    rows = x_st.shape[0]
    width = x_st.shape[1]
    block = HEAD
    own_l = lax.axis_index("local")
    own_n = lax.axis_index("node")
    peers = n_local + n_node
    entries = peers * CHUNK

    def load(r):
        copies = []
        spans = []
        for u in range(PAIR):
            j, to = r * PAIR + u, u * GW
            spans += [
                (q_hbm, j * (GROUP * HEAD), GROUP * HEAD, to),
                (g_hbm, j * (GROUP * HEAD), GROUP * HEAD, to + GROUP * HEAD),
                (kv_hbm, j * HEAD, HEAD, to + 2 * GROUP * HEAD),
                (kv_hbm, KEY_HEAD_WIDTH + j * HEAD, HEAD, to + (2 * GROUP + 1) * HEAD),
            ]
        for i, (src, at, size, to) in enumerate(spans):
            copies.append(
                pltpu.make_async_copy(
                    src.at[:, pl.ds(pl.multiple_of(at, HEAD), size)],
                    stage.at[r, :, to : to + size],
                    load_sem.at[r, i],
                )
            )
        return copies

    x_copy = pltpu.make_async_copy(x_hbm, x_st, xload_sem.at[0])
    down_copy = pltpu.make_async_copy(down_hbm, down_v, xload_sem.at[1])
    up_copy = pltpu.make_async_copy(up_hbm, up_ref, xload_sem.at[2])
    int_copies = [
        pltpu.make_async_copy(src, ints.at[i], int_sem.at[i])
        for i, src in enumerate((bl_hbm, bo_hbm, sn_hbm, so_hbm, pick_hbm, seg_hbm))
    ]
    for copy in int_copies:
        copy.start()

    barrier = pltpu.get_barrier_semaphore()
    for o in range(1, n_local):
        pl.semaphore_signal(
            barrier,
            inc=1,
            device_id={"local": lax.rem(own_l + o, n_local)},
            device_id_type=pl.DeviceIdType.MESH,
        )
    for o in range(1, n_node):
        pl.semaphore_signal(
            barrier,
            inc=1,
            device_id={"node": lax.rem(own_n + o, n_node)},
            device_id_type=pl.DeviceIdType.MESH,
        )

    def start_load(j, c):
        for copy in load(j):
            copy.start()
        return c

    lax.fori_loop(0, ROUNDS, start_load, 0)
    x_copy.start()
    down_copy.start()
    up_copy.start()
    for copy in int_copies:
        copy.wait()
    near_bin, near_off, far_bin, far_off = ints[0], ints[1], ints[2], ints[3]

    moved_in = near_bin != own_l
    moved_out = far_bin != own_n
    code = jnp.where(
        moved_in,
        near_bin * CAP + near_off,
        jnp.where(moved_out, (n_local + far_bin) * CAP + far_off, -1),
    )
    a_sub = iota((entries, rows), 0)
    hit = code == (a_sub // CHUNK) * CAP + a_sub % CAP
    for c in range(4):
        pack_hot[c] = jnp.where(hit & ((a_sub // CAP) % 4 == c), 1.0, 0.0).astype(BF16)
    pick = column(ints[4])
    own_hot[...] = jnp.where(pick == iota((rows, rows), 1), 1.0, 0.0).astype(BF16)
    a_lane = iota((rows, entries), 1)
    got = pick == rows + (a_lane // CHUNK) * CAP + a_lane % CAP
    for c in range(4):
        arr_hot[c] = jnp.where(got & ((a_lane // CAP) % 4 == c), 1.0, 0.0).astype(BF16)

    for slot in (own_l, n_local + own_n):
        arr_d[slot] = jnp.zeros(arr_d.shape[1:], BF16)
        arr_l[slot] = jnp.zeros(arr_l.shape[1:], BF16)

    def clear(j, c):
        for slot in (own_l, n_local + own_n):
            arr[j, slot] = jnp.zeros(arr.shape[2:], BF16)
        return c

    lax.fori_loop(0, ROUNDS, clear, 0)

    sum_peers = []
    if factor is not None:
        core, lx = lax.rem(own_l, 2), own_l // 2
        y, z = lax.rem(own_n, 2), own_n // 2
        n_x, n_z = n_local // 2, n_node // 2
        n_group = 2 * n_x
        own_g = y * n_x + lx
        sibling = {"local": lx * 2 + (1 - core), "node": own_n}
        group = []
        for o in range(1, n_group):
            g = lax.rem(own_g + o, n_group)
            to = {"local": lax.rem(g, n_x) * 2 + core, "node": z * 2 + g // n_x}
            group.append((g, to))
        far = []
        for o in range(1, n_z):
            t = lax.rem(z + o, n_z)
            far.append((t, {"local": own_l, "node": t * 2 + y}))
        sum_peers = [sibling] + [to for _, to in group] + [to for _, to in far]
        for to in sum_peers:
            pl.semaphore_signal(barrier, inc=1, device_id=to, device_id_type=pl.DeviceIdType.MESH)

    pl.semaphore_wait(barrier, n_local - 1 + n_node - 1 + len(sum_peers))

    def message(j, axis, o, src, dst):
        count, me, base = (n_local, own_l, 0) if axis == "local" else (n_node, own_n, n_local)
        to = lax.rem(me + o, count)
        return pltpu.make_async_remote_copy(
            src_ref=src.at[base + to],
            dst_ref=dst.at[base + me],
            send_sem=send_sem.at[j, base + to],
            recv_sem=recv_sem.at[j, base + me],
            device_id={axis: to},
            device_id_type=pl.DeviceIdType.MESH,
        )

    def arrival(j, axis, o, src, dst):
        count, me, base = (n_local, own_l, 0) if axis == "local" else (n_node, own_n, n_local)
        frm = lax.rem(me + count - o, count)
        return pltpu.make_async_remote_copy(
            src_ref=src.at[base + frm],
            dst_ref=dst.at[base + frm],
            send_sem=send_sem.at[j, base + frm],
            recv_sem=recv_sem.at[j, base + frm],
            device_id={axis: frm},
            device_id_type=pl.DeviceIdType.MESH,
        )

    hops = [("node", o) for o in range(1, n_node)] + [("local", o) for o in range(1, n_local)]

    def pack(j, carry):
        for copy in load(j):
            copy.wait()
        total = dot(pack_hot[0], stage[j, :, 0:GQ])
        for c in range(1, 4):
            total += dot(pack_hot[c], stage[j, :, c * GQ : (c + 1) * GQ])
        send[j] = total.astype(BF16).reshape(peers, CHUNK, GQ)
        for axis, o in hops:
            message(j, axis, o, send.at[j], arr.at[j]).start()
        return carry

    lax.fori_loop(0, ROUNDS, pack, 0)
    x_copy.wait()
    down_copy.wait()
    down_rows[...] = dot(x_st[...], down_v[...]).astype(BF16)
    send_d[...] = dot(pack_hot[0], down_rows[...]).astype(BF16).reshape(send_d.shape)
    for axis, o in hops:
        message(ROUNDS, axis, o, send_d, arr_d).start()

    seg_row = ints[5]
    seg_col = column(seg_row)
    allowed = (seg_col == seg_row) & (iota((rows, rows), 0) <= iota((rows, rows), 1))
    bias[...] = jnp.where(allowed, 0.0, -1e30)
    first = jnp.sum(jnp.where(seg_row < seg_col, 1.0, 0.0), axis=1, keepdims=True)
    position = iota((rows, HEAD), 0).astype(F32) - first
    lane = iota((rows, HEAD), 1)
    half = lane % (HEAD // 2)
    frequency = jnp.exp(half.astype(F32) * (-2.0 * math.log(ROPE_THETA) / HEAD))
    angles = position * frequency
    cos_v[...] = jnp.cos(angles)
    sin_v[...] = jnp.where(lane < HEAD // 2, jnp.sin(angles), -jnp.sin(angles))
    lift[...] = jnp.zeros_like(lift)

    def turn(i, carry):
        at = pl.multiple_of(i * HEAD, HEAD)
        x_turned[pl.ds(at, HEAD), :] = jnp.transpose(x_st[:, pl.ds(at, HEAD)])
        return carry

    lax.fori_loop(0, width // HEAD, turn, 0)
    up_copy.wait()

    def remote(src, dst, to_sem, from_sem, to):
        return pltpu.make_async_remote_copy(
            src_ref=src,
            dst_ref=dst,
            send_sem=to_sem,
            recv_sem=from_sem,
            device_id=to,
            device_id_type=pl.DeviceIdType.MESH,
        )

    def sums(own_lift):
        a_rows, b_rows = down_sum.shape[0], up_sum.shape[0]

        def pieces(t, g, at_core):
            part = (t * 2 + g // n_x) * n_local + lax.rem(g, n_x) * 2 + at_core
            a = dot(x_turned[pl.ds(pl.multiple_of(part * a_rows, 16), a_rows), :], own_lift)
            return a, dup_ref[pl.ds(pl.multiple_of(part * b_rows, 16), b_rows), :]

        order = [t for t, _ in far] + [z]
        copies = []
        for t in order:
            for g in range(n_group):
                a, b = pieces(t, g, 1 - core)
                send_a[t, g, :a_rows, :] = a.astype(BF16)
                send_a[t, g, a_rows:, :] = b.astype(BF16)
            copy = remote(send_a.at[t], recv_a.at[t], sem_a.at[0, t], sem_a.at[1, t], sibling)
            copy.start()
            copies.append(copy)
        for t in order:
            for g in range(n_group):
                a, b = pieces(t, g, core)
                own_part[t, g, :a_rows, :] = a
                own_part[t, g, a_rows:, :] = b
        for t, copy in zip(order, copies[:]):
            copy.wait_recv()
            for g, to in group:
                send_b[t, g] = (own_part[t, g] + recv_a[t, g].astype(F32)).astype(BF16)
                out = remote(
                    send_b.at[t, g],
                    recv_b.at[t, own_g],
                    sem_b.at[0, t, g],
                    sem_b.at[1, t, own_g],
                    to,
                )
                out.start()
                copies.append(out)
            mid[t] = own_part[t, own_g] + recv_a[t, own_g].astype(F32)
        for i, t in enumerate(order):
            total = mid[t]
            for g, to in group:
                remote(
                    send_b.at[t, g], recv_b.at[t, g], sem_b.at[0, t, g], sem_b.at[1, t, g], to
                ).wait_recv()
                total += recv_b[t, g].astype(F32)
            if i < len(far):
                send_c[t] = total.astype(BF16)
                out = remote(
                    send_c.at[t], recv_c.at[z], sem_c.at[0, t], sem_c.at[1, z], far[i][1]
                )
                out.start()
                copies.append(out)
            else:
                last[...] = total
        for t, to in far:
            remote(
                send_c.at[t], recv_c.at[t], sem_c.at[0, t], sem_c.at[1, t], to
            ).wait_recv()
            last[...] += recv_c[t].astype(F32)
        down_sum[...] = last[:a_rows, :] * factor
        up_sum[...] = last[a_rows:, :] * factor
        for copy in copies:
            copy.wait_send()

    scale = 1.0 / math.sqrt(HEAD)
    exp_scale = scale * math.log2(math.e)
    up_row = iota((2 * ADAPTER_RANK, HEAD), 0)

    def cot_copies(j):
        return (
            pltpu.make_async_copy(
                keys_out.at[j],
                cot_hbm.at[:, pl.ds(pl.multiple_of(j * HEAD, HEAD), HEAD)],
                out_sem.at[j, 0],
            ),
            pltpu.make_async_copy(
                vals_out.at[j],
                cot_hbm.at[:, pl.ds(pl.multiple_of(KEY_HEAD_WIDTH + j * HEAD, HEAD), HEAD)],
                out_sem.at[j, 1],
            ),
        )

    def head(r, carry):
        for axis, o in hops:
            arrival(r, axis, o, send.at[r], arr.at[r]).wait_recv()
        arrived = arr[r].reshape(entries, GQ)
        per = GQ // HEAD
        for c in range(4):
            part = dot(own_hot[...], stage[r, :, c * GQ : (c + 1) * GQ])
            part += dot(arr_hot[c], arrived)
            part = part.astype(BF16)
            for i in range(per):
                u, col = divmod(c * per + i, 2 * GROUP + 2)
                piece = part[:, i * HEAD : (i + 1) * HEAD]
                if col >= 2 * GROUP:
                    kvs[u, col - 2 * GROUP] = piece
                    continue
                dst, h = (qs, col) if col < GROUP else (gs, col - GROUP)
                for b in range(rows // block):
                    dst[u, b, h * block : (h + 1) * block, :] = piece[b * block : (b + 1) * block]
        for u in range(PAIR):
            one_head(r * PAIR + u, u)
        return carry

    def one_head(j, u):
        d_keys = [jnp.zeros((block, HEAD), F32)] * (rows // block)
        d_vals = [jnp.zeros((block, HEAD), F32)] * (rows // block)
        for b in range(rows // block):
            seen = (b + 1) * block
            scores = dot_t(kvs[u, 0, :seen, :], qs[u, b])
            prob_grads = dot_t(kvs[u, 1, :seen, :], gs[u, b])
            mask = bias[:seen, b * block : (b + 1) * block]
            for h in range(GROUP):
                cols = slice(h * block, (h + 1) * block)
                score = scores[:, cols] + mask
                top = jnp.max(score, axis=0, keepdims=True)
                weights = jnp.exp2((score - top) * exp_scale)
                probs = weights * (1.0 / jnp.sum(weights, axis=0, keepdims=True))
                prob_grad = prob_grads[:, cols]
                delta = jnp.sum(probs * prob_grad, axis=0, keepdims=True)
                probs_s[u, b, :seen, cols] = probs.astype(BF16)
                grads_s[u, b, :seen, cols] = (probs * (prob_grad - delta)).astype(BF16)
            d_val = dot(probs_s[u, b, :seen, :], gs[u, b])
            d_key = dot(grads_s[u, b, :seen, :], qs[u, b])
            for t in range(b + 1):
                d_vals[t] += d_val[t * block : (t + 1) * block]
                d_keys[t] += d_key[t * block : (t + 1) * block]
        d_key = jnp.concatenate(d_keys, axis=0)
        d_val = jnp.concatenate(d_vals, axis=0)
        d_key = d_key * scale
        d_key = d_key * cos_v[...] + pltpu.roll(d_key, HEAD // 2, 1) * sin_v[...]
        key_low = d_key.astype(BF16)
        val_low = d_val.astype(BF16)
        keys_out[j] = key_low
        vals_out[j] = val_low
        for copy in cot_copies(j):
            copy.start()
        up = up_ref[:, pl.ds(pl.multiple_of(j * HEAD, HEAD), HEAD)].astype(F32)
        up_key = jnp.where(up_row < ADAPTER_RANK, up, 0.0).astype(BF16)
        up_val = jnp.where(up_row < ADAPTER_RANK, 0.0, up).astype(BF16)
        lift[...] += dot_t(key_low, up_key) + dot_t(val_low, up_val)

    lax.fori_loop(0, ROUNDS, head, 0)

    lift_low = lift[...].astype(BF16)
    send_l[...] = dot_l(arr_hot[0], lift_low).astype(BF16).reshape(send_l.shape)
    for axis, o in hops:
        message(ROUNDS + 1, axis, o, send_l, arr_l).start()

    for axis, o in hops:
        arrival(ROUNDS, axis, o, send_d, arr_d).wait_recv()
    down_out = dot(own_hot[...], down_rows[...])
    down_out += dot(arr_hot[0], arr_d[...].reshape(entries, HEAD))
    down_low = down_out.astype(BF16)
    down_lane = iota((HEAD, 2 * ADAPTER_RANK), 1) < ADAPTER_RANK

    def up_grad(j, carry):
        from_key = dot_l(keys_out[j], down_low)
        from_val = dot_l(vals_out[j], down_low)
        dup_ref[pl.ds(pl.multiple_of(j * HEAD, HEAD), HEAD), :] = jnp.where(
            down_lane, from_key, from_val
        )
        return carry

    lax.fori_loop(0, KV_HEADS, up_grad, 0)

    own_lift = dot_l(own_hot[...], lift_low)
    for axis, o in hops:
        arrival(ROUNDS + 1, axis, o, send_l, arr_l).wait_recv()
    own_lift += dot_l(pack_hot[0], arr_l[...].reshape(entries, HEAD))
    own_lift = own_lift.astype(BF16)
    if factor is None:
        span = width // 8
        for c in range(8):
            at = slice(c * span, (c + 1) * span)
            ddown_ref[at, :] = dot(x_turned[at, :], own_lift)
    else:
        sums(own_lift)

    def finish(j, carry):
        for copy in cot_copies(j):
            copy.wait()
        return carry

    lax.fori_loop(0, KV_HEADS, finish, 0)

    def sent(r, carry):
        for axis, o in hops:
            message(r, axis, o, send.at[r], arr.at[r]).wait_send()
        return carry

    lax.fori_loop(0, ROUNDS, sent, 0)
    for axis, o in hops:
        message(ROUNDS, axis, o, send_d, arr_d).wait_send()
        message(ROUNDS + 1, axis, o, send_l, arr_l).wait_send()


def sum_kernel(
    n_local,
    n_node,
    factor,
    a_ref,
    b_ref,
    a_out,
    b_out,
    send_a,
    recv_a,
    send_b,
    recv_b,
    send_c,
    recv_c,
    mid,
    last,
    sem_a,
    sem_b,
    sem_c,
):
    n_x, n_z = n_local // 2, n_node // 2
    own_l = lax.axis_index("local")
    own_n = lax.axis_index("node")
    core, lx = lax.rem(own_l, 2), own_l // 2
    y, z = lax.rem(own_n, 2), own_n // 2
    a_rows = a_ref.shape[4]
    n_group = 2 * n_x
    own_g = y * n_x + lx
    mesh_id = pl.DeviceIdType.MESH

    sibling = {"local": lx * 2 + (1 - core), "node": own_n}
    group = []
    for o in range(1, n_group):
        g = lax.rem(own_g + o, n_group)
        group.append((g, {"local": lax.rem(g, n_x) * 2 + core, "node": z * 2 + g // n_x}))
    far = []
    for o in range(1, n_z):
        t = lax.rem(z + o, n_z)
        far.append((t, {"local": own_l, "node": t * 2 + y}))

    barrier = pltpu.get_barrier_semaphore()
    targets = [sibling] + [d for _, d in group] + [d for _, d in far]
    for d in targets:
        pl.semaphore_signal(barrier, inc=1, device_id=d, device_id_type=mesh_id)

    for yy in range(2):
        for xx in range(n_x):
            g = yy * n_x + xx
            send_a[g, :, :a_rows, :] = a_ref[:, yy, xx, 1 - core].astype(BF16)
            send_a[g, :, a_rows:, :] = b_ref[:, yy, xx, 1 - core].astype(BF16)
    pl.semaphore_wait(barrier, len(targets))
    copies_a = []
    for o in range(n_group):
        g = lax.rem(own_g + 1 + o, n_group)
        copy = pltpu.make_async_remote_copy(
            src_ref=send_a.at[g],
            dst_ref=recv_a.at[g],
            send_sem=sem_a.at[0, g],
            recv_sem=sem_a.at[1, g],
            device_id=sibling,
            device_id_type=mesh_id,
        )
        copy.start()
        copies_a.append((g, copy))

    copies_b = []
    for o in range(n_group):
        g, copy = copies_a[o]
        copy.wait_recv()
        yy, xx = g // n_x, lax.rem(g, n_x)
        top = a_ref[:, yy, xx, core] + recv_a[g, :, :a_rows, :].astype(F32)
        low = b_ref[:, yy, xx, core] + recv_a[g, :, a_rows:, :].astype(F32)
        if o < n_group - 1:
            send_b[g, :, :a_rows, :] = top.astype(BF16)
            send_b[g, :, a_rows:, :] = low.astype(BF16)
            out = pltpu.make_async_remote_copy(
                src_ref=send_b.at[g],
                dst_ref=recv_b.at[own_g],
                send_sem=sem_b.at[0, g],
                recv_sem=sem_b.at[1, own_g],
                device_id=group[o][1],
                device_id_type=mesh_id,
            )
            out.start()
            copies_b.append(out)
        else:
            mid[:, :a_rows, :] = top
            mid[:, a_rows:, :] = low

    for g, d in group:
        pltpu.make_async_remote_copy(
            src_ref=send_b.at[g],
            dst_ref=recv_b.at[g],
            send_sem=sem_b.at[0, g],
            recv_sem=sem_b.at[1, g],
            device_id=d,
            device_id_type=mesh_id,
        ).wait_recv()
        mid[...] += recv_b[g].astype(F32)

    copies_c = []
    for t, d in far:
        send_c[t] = mid[t].astype(BF16)
        out = pltpu.make_async_remote_copy(
            src_ref=send_c.at[t],
            dst_ref=recv_c.at[z],
            send_sem=sem_c.at[0, t],
            recv_sem=sem_c.at[1, z],
            device_id=d,
            device_id_type=mesh_id,
        )
        out.start()
        copies_c.append(out)
    last[...] = mid[z]
    for t, d in far:
        pltpu.make_async_remote_copy(
            src_ref=send_c.at[t],
            dst_ref=recv_c.at[t],
            send_sem=sem_c.at[0, t],
            recv_sem=sem_c.at[1, t],
            device_id=d,
            device_id_type=mesh_id,
        ).wait_recv()
        last[...] += recv_c[t].astype(F32)
    a_out[...] = last[:a_rows, :] * factor
    b_out[...] = last[a_rows:, :] * factor
    for _, copy in copies_a:
        copy.wait_send()
    for copy in copies_b + copies_c:
        copy.wait_send()


def factor_sums(n_local, n_node, factor, a, b):
    n_x, n_z = n_local // 2, n_node // 2
    n_dev = n_local * n_node

    def lay(v):
        size = v.shape[0] // n_dev
        padded = -(-size // 16) * 16
        v = v.reshape(n_dev, size, v.shape[1])
        if padded != size:
            v = jnp.pad(v, ((0, 0), (0, padded - size), (0, 0)))
        return v.reshape(n_z, 2, n_x, 2, padded, v.shape[2]), size, padded

    a, a_size, a_rows = lay(a)
    b, b_size, b_rows = lay(b)
    rows = a_rows + b_rows
    wide = a.shape[-1]
    n_group = 2 * n_x
    vmem = pl.BlockSpec(memory_space=pltpu.VMEM)
    a_out, b_out = pl.pallas_call(
        functools.partial(sum_kernel, n_local, n_node, factor),
        out_shape=(
            jax.ShapeDtypeStruct((a_rows, wide), F32),
            jax.ShapeDtypeStruct((b_rows, wide), F32),
        ),
        in_specs=[vmem, vmem],
        out_specs=(vmem, vmem),
        scratch_shapes=[
            pltpu.VMEM((n_group, n_z, rows, wide), BF16),
            pltpu.VMEM((n_group, n_z, rows, wide), BF16),
            pltpu.VMEM((n_group, n_z, rows, wide), BF16),
            pltpu.VMEM((n_group, n_z, rows, wide), BF16),
            pltpu.VMEM((n_z, rows, wide), BF16),
            pltpu.VMEM((n_z, rows, wide), BF16),
            pltpu.VMEM((n_z, rows, wide), F32),
            pltpu.VMEM((rows, wide), F32),
            pltpu.SemaphoreType.DMA((2, n_group)),
            pltpu.SemaphoreType.DMA((2, n_group)),
            pltpu.SemaphoreType.DMA((2, n_z)),
        ],
        compiler_params=pltpu.CompilerParams(
            collective_id=1, has_side_effects=True, vmem_limit_bytes=48 * 2**20
        ),
        name="factor_sums",
    )(a, b)
    return a_out[:a_size], b_out[:b_size]


def local(n_local, n_node, *args):
    activations, queries, rotated_key_value, attention_out_grad, adapter_down, adapter_up = args[:6]
    rows, width = activations.shape
    peers = n_local + n_node
    entries = peers * CHUNK
    vmem = pl.BlockSpec(memory_space=pltpu.VMEM)
    hbm = pl.BlockSpec(memory_space=pl.ANY)
    n_dev = n_local * n_node
    wide = 2 * ADAPTER_RANK
    factor = 1.0 / math.sqrt(rows * n_dev)
    a_rows, b_rows = width // n_dev, KEY_HEAD_WIDTH // n_dev
    fused = a_rows % 16 == 0 and b_rows % 16 == 0
    shrink = n_dev if fused else 1
    extra = []
    if fused:
        n_z, n_group, size = n_node // 2, n_local, a_rows + b_rows
        slab = (n_z, n_group, size, wide)
        extra = [
            pltpu.VMEM((KEY_HEAD_WIDTH, wide), F32),
            pltpu.VMEM(slab, BF16),
            pltpu.VMEM(slab, BF16),
            pltpu.VMEM(slab, BF16),
            pltpu.VMEM(slab, BF16),
            pltpu.VMEM((n_z, size, wide), BF16),
            pltpu.VMEM((n_z, size, wide), BF16),
            pltpu.VMEM(slab, F32),
            pltpu.VMEM((n_z, size, wide), F32),
            pltpu.VMEM((size, wide), F32),
            pltpu.SemaphoreType.DMA((2, n_z)),
            pltpu.SemaphoreType.DMA((2, n_z, n_group)),
            pltpu.SemaphoreType.DMA((2, n_z)),
        ]
    cotangent, down_grad, up_grad = pl.pallas_call(
        functools.partial(main_kernel, n_local, n_node, factor if fused else None),
        out_shape=(
            jax.ShapeDtypeStruct((rows, 2 * KEY_HEAD_WIDTH), BF16),
            jax.ShapeDtypeStruct((width // shrink, wide), F32),
            jax.ShapeDtypeStruct((KEY_HEAD_WIDTH // shrink, wide), F32),
        ),
        in_specs=[hbm] * 12,
        out_specs=(hbm, vmem, vmem),
        scratch_shapes=[
            pltpu.VMEM((6, 1, rows), jnp.int32),
            pltpu.VMEM(adapter_up.shape, BF16),
            pltpu.VMEM((ROUNDS, rows, PAIR * GW), BF16),
            pltpu.VMEM((rows, width), BF16),
            pltpu.VMEM((width, rows), BF16),
            pltpu.VMEM((width, 2 * ADAPTER_RANK), BF16),
            pltpu.VMEM((rows, 2 * ADAPTER_RANK), BF16),
            pltpu.VMEM((ROUNDS, peers, CHUNK, GQ), BF16),
            pltpu.VMEM((peers, CHUNK, 2 * ADAPTER_RANK), BF16),
            pltpu.VMEM((peers, CHUNK, 2 * ADAPTER_RANK), BF16),
            pltpu.VMEM((ROUNDS, peers, CHUNK, GQ), BF16),
            pltpu.VMEM((peers, CHUNK, 2 * ADAPTER_RANK), BF16),
            pltpu.VMEM((peers, CHUNK, 2 * ADAPTER_RANK), BF16),
            pltpu.VMEM((4, entries, rows), BF16),
            pltpu.VMEM((rows, rows), BF16),
            pltpu.VMEM((4, rows, entries), BF16),
            pltpu.VMEM((rows, rows), F32),
            pltpu.VMEM((rows, HEAD), F32),
            pltpu.VMEM((rows, HEAD), F32),
            pltpu.VMEM((PAIR, rows // HEAD, GROUP * HEAD, HEAD), BF16),
            pltpu.VMEM((PAIR, rows // HEAD, GROUP * HEAD, HEAD), BF16),
            pltpu.VMEM((PAIR, 2, rows, HEAD), BF16),
            pltpu.VMEM((PAIR, rows // HEAD, rows, GROUP * HEAD), BF16),
            pltpu.VMEM((PAIR, rows // HEAD, rows, GROUP * HEAD), BF16),
            pltpu.VMEM((KV_HEADS, rows, HEAD), BF16),
            pltpu.VMEM((KV_HEADS, rows, HEAD), BF16),
            pltpu.VMEM((rows, 2 * ADAPTER_RANK), F32),
            pltpu.SemaphoreType.DMA((6,)),
            pltpu.SemaphoreType.DMA((ROUNDS, 4 * PAIR)),
            pltpu.SemaphoreType.DMA((3,)),
            pltpu.SemaphoreType.DMA((KV_HEADS, 2)),
            pltpu.SemaphoreType.DMA((ROUNDS + 2, peers)),
            pltpu.SemaphoreType.DMA((ROUNDS + 2, peers)),
            *extra,
        ],
        compiler_params=pltpu.CompilerParams(
            collective_id=0, has_side_effects=True, vmem_limit_bytes=60 * 2**20
        ),
        name="exchange_attention",
    )(*args)
    if fused:
        return cotangent, down_grad, up_grad
    down_sum, up_sum = factor_sums(n_local, n_node, factor, down_grad, up_grad)
    return cotangent, down_sum, up_sum


def solution(mesh):
    placed = (P(("node", "local"), None),) * 4 + (P(),) * 2 + (P(("node", "local"), None),) * 6
    return jax.shard_map(
        functools.partial(local, mesh.shape["local"], mesh.shape["node"]),
        mesh=mesh,
        in_specs=placed,
        out_specs=(P(("node", "local"), None),) * 3,
        check_vma=False,
    )
```

```python
import functools
import math

import jax
import jax.numpy as jnp
import numpy as np
from jax import lax
from jax.experimental import pallas as pl
from jax.experimental.pallas import tpu as pltpu
from jax.sharding import PartitionSpec as P

KV_HEADS = 8
HEAD = 128
ADAPTER_RANK = 64
CAP = 4
GROUP = 5
KEY_HEAD_WIDTH = 1024
CHUNK = 16
GW = (2 * GROUP + 2) * HEAD
PAIR = 2
ROUNDS = KV_HEADS // PAIR
GQ = PAIR * GW // 4
ROPE_THETA = 1000000.0
F32 = jnp.float32
BF16 = jnp.bfloat16


def dot(a, b):
    return jnp.dot(a, b, preferred_element_type=F32)


def dot_t(a, b):
    return lax.dot_general(a, b, (((1,), (1,)), ((), ())), preferred_element_type=F32)


def dot_l(a, b):
    return lax.dot_general(a, b, (((0,), (0,)), ((), ())), preferred_element_type=F32)


def iota(shape, axis):
    return lax.broadcasted_iota(jnp.int32, shape, axis)


def column(row):
    rows = row.shape[1]
    wide = jnp.broadcast_to(row.astype(F32), (128, rows))
    return jnp.transpose(wide)[:, 0:1].astype(jnp.int32)


def main_kernel(
    n_local,
    n_node,
    factor,
    x_hbm,
    q_hbm,
    kv_hbm,
    g_hbm,
    down_hbm,
    up_hbm,
    bl_hbm,
    bo_hbm,
    sn_hbm,
    so_hbm,
    pick_hbm,
    seg_hbm,
    cot_hbm,
    *rest,
):
    if factor is None:
        ddown_ref, dup_ref = rest[:2]
    else:
        down_sum, up_sum = rest[:2]
        dup_ref, send_a, recv_a, send_b, recv_b, send_c, recv_c = rest[-13:-6]
        own_part, mid, last, sem_a, sem_b, sem_c = rest[-6:]
    (
        ints,
        up_ref,
        stage,
        x_st,
        x_turned,
        down_v,
        down_rows,
        send,
        send_d,
        send_l,
        arr,
        arr_d,
        arr_l,
        pack_hot,
        own_hot,
        arr_hot,
        bias,
        cos_v,
        sin_v,
        qs,
        gs,
        kvs,
        probs_s,
        grads_s,
        keys_out,
        vals_out,
        lift,
        int_sem,
        load_sem,
        xload_sem,
        out_sem,
        send_sem,
        recv_sem,
    ) = rest[2:35]
    rows = x_st.shape[0]
    width = x_st.shape[1]
    block = HEAD
    own_l = lax.axis_index("local")
    own_n = lax.axis_index("node")
    peers = n_local + n_node
    entries = peers * CHUNK

    def load(r):
        copies = []
        spans = []
        for u in range(PAIR):
            j, to = r * PAIR + u, u * GW
            spans += [
                (q_hbm, j * (GROUP * HEAD), GROUP * HEAD, to),
                (g_hbm, j * (GROUP * HEAD), GROUP * HEAD, to + GROUP * HEAD),
                (kv_hbm, j * HEAD, HEAD, to + 2 * GROUP * HEAD),
                (kv_hbm, KEY_HEAD_WIDTH + j * HEAD, HEAD, to + (2 * GROUP + 1) * HEAD),
            ]
        for i, (src, at, size, to) in enumerate(spans):
            copies.append(
                pltpu.make_async_copy(
                    src.at[:, pl.ds(pl.multiple_of(at, HEAD), size)],
                    stage.at[r, :, to : to + size],
                    load_sem.at[r, i],
                )
            )
        return copies

    x_copy = pltpu.make_async_copy(x_hbm, x_st, xload_sem.at[0])
    down_copy = pltpu.make_async_copy(down_hbm, down_v, xload_sem.at[1])
    up_copy = pltpu.make_async_copy(up_hbm, up_ref, xload_sem.at[2])
    int_copies = [
        pltpu.make_async_copy(src, ints.at[i], int_sem.at[i])
        for i, src in enumerate((bl_hbm, bo_hbm, sn_hbm, so_hbm, pick_hbm, seg_hbm))
    ]
    for copy in int_copies:
        copy.start()

    barrier = pltpu.get_barrier_semaphore()
    for o in range(1, n_local):
        pl.semaphore_signal(
            barrier,
            inc=1,
            device_id={"local": lax.rem(own_l + o, n_local)},
            device_id_type=pl.DeviceIdType.MESH,
        )
    for o in range(1, n_node):
        pl.semaphore_signal(
            barrier,
            inc=1,
            device_id={"node": lax.rem(own_n + o, n_node)},
            device_id_type=pl.DeviceIdType.MESH,
        )

    def start_load(j, c):
        for copy in load(j):
            copy.start()
        return c

    lax.fori_loop(0, 2, start_load, 0)
    for copy in int_copies:
        copy.wait()
    near_bin, near_off, far_bin, far_off = ints[0], ints[1], ints[2], ints[3]

    moved_in = near_bin != own_l
    moved_out = far_bin != own_n
    code = jnp.where(
        moved_in,
        near_bin * CAP + near_off,
        jnp.where(moved_out, (n_local + far_bin) * CAP + far_off, -1),
    )
    a_sub = iota((entries, rows), 0)
    hit = code == (a_sub >> 4) * CAP + (a_sub & 3)
    for c in range(4):
        pack_hot[c] = jnp.where(hit & (((a_sub >> 2) & 3) == c), 1.0, 0.0).astype(BF16)

    for slot in (own_l, n_local + own_n):
        arr_d[slot] = jnp.zeros(arr_d.shape[1:], BF16)
        arr_l[slot] = jnp.zeros(arr_l.shape[1:], BF16)

    def clear(j, c):
        for slot in (own_l, n_local + own_n):
            arr[j, slot] = jnp.zeros(arr.shape[2:], BF16)
        return c

    lax.fori_loop(0, ROUNDS, clear, 0)

    sum_peers = []
    if factor is not None:
        core, lx = lax.rem(own_l, 2), own_l // 2
        y, z = lax.rem(own_n, 2), own_n // 2
        n_x, n_z = n_local // 2, n_node // 2
        n_group = 2 * n_x
        own_g = y * n_x + lx
        sibling = {"local": lx * 2 + (1 - core), "node": own_n}
        group = []
        for o in range(1, n_group):
            g = lax.rem(own_g + o, n_group)
            to = {"local": lax.rem(g, n_x) * 2 + core, "node": z * 2 + g // n_x}
            group.append((g, to))
        far = []
        for o in range(1, n_z):
            t = lax.rem(z + o, n_z)
            far.append((t, {"local": own_l, "node": t * 2 + y}))
        sum_peers = [sibling] + [to for _, to in group] + [to for _, to in far]
        for to in sum_peers:
            pl.semaphore_signal(barrier, inc=1, device_id=to, device_id_type=pl.DeviceIdType.MESH)

    pl.semaphore_wait(barrier, n_local - 1 + n_node - 1 + len(sum_peers))

    def message(j, axis, o, src, dst):
        count, me, base = (n_local, own_l, 0) if axis == "local" else (n_node, own_n, n_local)
        to = lax.rem(me + o, count)
        return pltpu.make_async_remote_copy(
            src_ref=src.at[base + to],
            dst_ref=dst.at[base + me],
            send_sem=send_sem.at[j, base + to],
            recv_sem=recv_sem.at[j, base + me],
            device_id={axis: to},
            device_id_type=pl.DeviceIdType.MESH,
        )

    def arrival(j, axis, o, src, dst):
        count, me, base = (n_local, own_l, 0) if axis == "local" else (n_node, own_n, n_local)
        frm = lax.rem(me + count - o, count)
        return pltpu.make_async_remote_copy(
            src_ref=src.at[base + frm],
            dst_ref=dst.at[base + frm],
            send_sem=send_sem.at[j, base + frm],
            recv_sem=recv_sem.at[j, base + frm],
            device_id={axis: frm},
            device_id_type=pl.DeviceIdType.MESH,
        )

    hops = [("node", o) for o in range(1, n_node)] + [("local", o) for o in range(1, n_local)]

    def pack(j, carry):
        for copy in load(j):
            copy.wait()

        @pl.when(j + 2 < ROUNDS)
        def _():
            start_load(j + 2, 0)

        @pl.when(j + 2 == ROUNDS)
        def _():
            x_copy.start()
            down_copy.start()
            up_copy.start()

        total = dot(pack_hot[0], stage[j, :, 0:GQ])
        for c in range(1, 4):
            total += dot(pack_hot[c], stage[j, :, c * GQ : (c + 1) * GQ])
        send[j] = total.astype(BF16).reshape(peers, CHUNK, GQ)
        for axis, o in hops:
            message(j, axis, o, send.at[j], arr.at[j]).start()
        return carry

    lax.fori_loop(0, ROUNDS, pack, 0)

    pick = column(ints[4])
    own_hot[...] = jnp.where(pick == iota((rows, rows), 1), 1.0, 0.0).astype(BF16)
    a_lane = iota((rows, entries), 1)
    got = pick == rows + (a_lane >> 4) * CAP + (a_lane & 3)
    for c in range(4):
        arr_hot[c] = jnp.where(got & (((a_lane >> 2) & 3) == c), 1.0, 0.0).astype(BF16)

    x_copy.wait()
    down_copy.wait()
    down_rows[...] = dot(x_st[...], down_v[...]).astype(BF16)
    send_d[...] = dot(pack_hot[0], down_rows[...]).astype(BF16).reshape(send_d.shape)
    for axis, o in hops:
        message(ROUNDS, axis, o, send_d, arr_d).start()

    seg_row = ints[5]
    seg_col = column(seg_row)
    allowed = (seg_col == seg_row) & (iota((rows, rows), 0) <= iota((rows, rows), 1))
    bias[...] = jnp.where(allowed, 0.0, -1e30)
    first = jnp.sum(jnp.where(seg_row < seg_col, 1.0, 0.0), axis=1, keepdims=True)
    position = iota((rows, HEAD), 0).astype(F32) - first
    lane = iota((rows, HEAD), 1)
    half = lane % (HEAD // 2)
    frequency = jnp.exp(half.astype(F32) * (-2.0 * math.log(ROPE_THETA) / HEAD))
    angles = position * frequency
    cos_v[...] = jnp.cos(angles)
    sin_v[...] = jnp.where(lane < HEAD // 2, jnp.sin(angles), -jnp.sin(angles))
    lift[...] = jnp.zeros_like(lift)

    def turn(i, carry):
        at = pl.multiple_of(i * HEAD, HEAD)
        x_turned[pl.ds(at, HEAD), :] = jnp.transpose(x_st[:, pl.ds(at, HEAD)])
        return carry

    lax.fori_loop(0, width // HEAD, turn, 0)
    up_copy.wait()

    def remote(src, dst, to_sem, from_sem, to):
        return pltpu.make_async_remote_copy(
            src_ref=src,
            dst_ref=dst,
            send_sem=to_sem,
            recv_sem=from_sem,
            device_id=to,
            device_id_type=pl.DeviceIdType.MESH,
        )

    def sums(own_lift):
        a_rows, b_rows = down_sum.shape[0], up_sum.shape[0]

        slab_rows = 2 * n_group * a_rows

        def up_piece(t, g, at_core):
            part = (t * 2 + g // n_x) * n_local + lax.rem(g, n_x) * 2 + at_core
            return dup_ref[pl.ds(pl.multiple_of(part * b_rows, 16), b_rows), :]

        order = [t for t, _ in far] + [z]
        copies = []
        for t in order:
            slab = dot(x_turned[pl.ds(pl.multiple_of(t * slab_rows, 16), slab_rows), :], own_lift)
            own_part[t] = slab.reshape(2 * n_group, a_rows, slab.shape[1])
            for g in range(n_group):
                send_a[t, g, :a_rows, :] = own_part[t, g * 2 + 1 - core].astype(BF16)
                send_a[t, g, a_rows:, :] = up_piece(t, g, 1 - core).astype(BF16)
            copy = remote(send_a.at[t], recv_a.at[t], sem_a.at[0, t], sem_a.at[1, t], sibling)
            copy.start()
            copies.append(copy)
        for t, copy in zip(order, copies[:]):
            copy.wait_recv()
            for g, to in group:
                got = recv_a[t, g].astype(F32)
                a = own_part[t, g * 2 + core] + got[:a_rows]
                b = up_piece(t, g, core) + got[a_rows:]
                send_b[t, g, :a_rows, :] = a.astype(BF16)
                send_b[t, g, a_rows:, :] = b.astype(BF16)
                out = remote(
                    send_b.at[t, g],
                    recv_b.at[t, own_g],
                    sem_b.at[0, t, g],
                    sem_b.at[1, t, own_g],
                    to,
                )
                out.start()
                copies.append(out)
            got = recv_a[t, own_g].astype(F32)
            mid[t, :a_rows, :] = own_part[t, own_g * 2 + core] + got[:a_rows]
            mid[t, a_rows:, :] = up_piece(t, own_g, core) + got[a_rows:]
        for i, t in enumerate(order):
            total = mid[t]
            for g, to in group:
                remote(
                    send_b.at[t, g], recv_b.at[t, g], sem_b.at[0, t, g], sem_b.at[1, t, g], to
                ).wait_recv()
                total += recv_b[t, g].astype(F32)
            if i < len(far):
                send_c[t] = total.astype(BF16)
                out = remote(
                    send_c.at[t], recv_c.at[z], sem_c.at[0, t], sem_c.at[1, z], far[i][1]
                )
                out.start()
                copies.append(out)
            else:
                last[...] = total
        for t, to in far:
            remote(
                send_c.at[t], recv_c.at[t], sem_c.at[0, t], sem_c.at[1, t], to
            ).wait_recv()
            last[...] += recv_c[t].astype(F32)
        down_sum[...] = last[:a_rows, :] * factor
        up_sum[...] = last[a_rows:, :] * factor
        for copy in copies:
            copy.wait_send()

    scale = 1.0 / math.sqrt(HEAD)
    exp_scale = scale * math.log2(math.e)
    up_row = iota((2 * ADAPTER_RANK, HEAD), 0)

    def cot_copies(j):
        return (
            pltpu.make_async_copy(
                keys_out.at[j],
                cot_hbm.at[:, pl.ds(pl.multiple_of(j * HEAD, HEAD), HEAD)],
                out_sem.at[j, 0],
            ),
            pltpu.make_async_copy(
                vals_out.at[j],
                cot_hbm.at[:, pl.ds(pl.multiple_of(KEY_HEAD_WIDTH + j * HEAD, HEAD), HEAD)],
                out_sem.at[j, 1],
            ),
        )

    def head(r, carry):
        for axis, o in hops:
            arrival(r, axis, o, send.at[r], arr.at[r]).wait_recv()
        arrived = arr[r].reshape(entries, GQ)
        per = GQ // HEAD
        for c in range(4):
            part = dot(own_hot[...], stage[r, :, c * GQ : (c + 1) * GQ])
            part += dot(arr_hot[c], arrived)
            part = part.astype(BF16)
            for i in range(per):
                u, col = divmod(c * per + i, 2 * GROUP + 2)
                piece = part[:, i * HEAD : (i + 1) * HEAD]
                if col >= 2 * GROUP:
                    kvs[u, col - 2 * GROUP] = piece
                    continue
                dst, h = (qs, col) if col < GROUP else (gs, col - GROUP)
                for b in range(rows // block):
                    dst[u, b, h * block : (h + 1) * block, :] = piece[b * block : (b + 1) * block]
        for u in range(PAIR):
            one_head(r * PAIR + u, u)
        return carry

    def one_head(j, u):
        d_keys = [jnp.zeros((block, HEAD), F32)] * (rows // block)
        d_vals = [jnp.zeros((block, HEAD), F32)] * (rows // block)
        for b in range(rows // block):
            seen = (b + 1) * block
            scores = dot_t(kvs[u, 0, :seen, :], qs[u, b])
            prob_grads = dot_t(kvs[u, 1, :seen, :], gs[u, b])
            mask = bias[:seen, b * block : (b + 1) * block]
            for h in range(GROUP):
                cols = slice(h * block, (h + 1) * block)
                score = scores[:, cols] + mask
                top = jnp.max(score, axis=0, keepdims=True)
                weights = jnp.exp2((score - top) * exp_scale)
                probs = weights * (1.0 / jnp.sum(weights, axis=0, keepdims=True))
                prob_grad = prob_grads[:, cols]
                delta = jnp.sum(probs * prob_grad, axis=0, keepdims=True)
                probs_s[u, b, :seen, cols] = probs.astype(BF16)
                grads_s[u, b, :seen, cols] = (probs * (prob_grad - delta)).astype(BF16)
            d_val = dot(probs_s[u, b, :seen, :], gs[u, b])
            d_key = dot(grads_s[u, b, :seen, :], qs[u, b])
            for t in range(b + 1):
                d_vals[t] += d_val[t * block : (t + 1) * block]
                d_keys[t] += d_key[t * block : (t + 1) * block]
        d_key = jnp.concatenate(d_keys, axis=0)
        d_val = jnp.concatenate(d_vals, axis=0)
        d_key = d_key * scale
        d_key = d_key * cos_v[...] + pltpu.roll(d_key, HEAD // 2, 1) * sin_v[...]
        key_low = d_key.astype(BF16)
        val_low = d_val.astype(BF16)
        keys_out[j] = key_low
        vals_out[j] = val_low
        for copy in cot_copies(j):
            copy.start()
        up = up_ref[:, pl.ds(pl.multiple_of(j * HEAD, HEAD), HEAD)].astype(F32)
        up_key = jnp.where(up_row < ADAPTER_RANK, up, 0.0).astype(BF16)
        up_val = jnp.where(up_row < ADAPTER_RANK, 0.0, up).astype(BF16)
        lift[...] += dot_t(key_low, up_key) + dot_t(val_low, up_val)

    lax.fori_loop(0, ROUNDS, head, 0)

    lift_low = lift[...].astype(BF16)
    send_l[...] = dot_l(arr_hot[0], lift_low).astype(BF16).reshape(send_l.shape)
    for axis, o in hops:
        message(ROUNDS + 1, axis, o, send_l, arr_l).start()

    for axis, o in hops:
        arrival(ROUNDS, axis, o, send_d, arr_d).wait_recv()
    down_out = dot(own_hot[...], down_rows[...])
    down_out += dot(arr_hot[0], arr_d[...].reshape(entries, HEAD))
    down_low = down_out.astype(BF16)
    down_lane = iota((HEAD, 2 * ADAPTER_RANK), 1) < ADAPTER_RANK

    def up_grad(j, carry):
        from_key = dot_l(keys_out[j], down_low)
        from_val = dot_l(vals_out[j], down_low)
        dup_ref[pl.ds(pl.multiple_of(j * HEAD, HEAD), HEAD), :] = jnp.where(
            down_lane, from_key, from_val
        )
        return carry

    lax.fori_loop(0, KV_HEADS, up_grad, 0)

    own_lift = dot_l(own_hot[...], lift_low)
    for axis, o in hops:
        arrival(ROUNDS + 1, axis, o, send_l, arr_l).wait_recv()
    own_lift += dot_l(pack_hot[0], arr_l[...].reshape(entries, HEAD))
    own_lift = own_lift.astype(BF16)
    if factor is None:
        span = width // 8
        for c in range(8):
            at = slice(c * span, (c + 1) * span)
            ddown_ref[at, :] = dot(x_turned[at, :], own_lift)
    else:
        sums(own_lift)

    def finish(j, carry):
        for copy in cot_copies(j):
            copy.wait()
        return carry

    lax.fori_loop(0, KV_HEADS, finish, 0)

    def sent(r, carry):
        for axis, o in hops:
            message(r, axis, o, send.at[r], arr.at[r]).wait_send()
        return carry

    lax.fori_loop(0, ROUNDS, sent, 0)
    for axis, o in hops:
        message(ROUNDS, axis, o, send_d, arr_d).wait_send()
        message(ROUNDS + 1, axis, o, send_l, arr_l).wait_send()


def sum_kernel(
    n_local,
    n_node,
    factor,
    a_ref,
    b_ref,
    a_out,
    b_out,
    send_a,
    recv_a,
    send_b,
    recv_b,
    send_c,
    recv_c,
    mid,
    last,
    sem_a,
    sem_b,
    sem_c,
):
    n_x, n_z = n_local // 2, n_node // 2
    own_l = lax.axis_index("local")
    own_n = lax.axis_index("node")
    core, lx = lax.rem(own_l, 2), own_l // 2
    y, z = lax.rem(own_n, 2), own_n // 2
    a_rows = a_ref.shape[4]
    n_group = 2 * n_x
    own_g = y * n_x + lx
    mesh_id = pl.DeviceIdType.MESH

    sibling = {"local": lx * 2 + (1 - core), "node": own_n}
    group = []
    for o in range(1, n_group):
        g = lax.rem(own_g + o, n_group)
        group.append((g, {"local": lax.rem(g, n_x) * 2 + core, "node": z * 2 + g // n_x}))
    far = []
    for o in range(1, n_z):
        t = lax.rem(z + o, n_z)
        far.append((t, {"local": own_l, "node": t * 2 + y}))

    barrier = pltpu.get_barrier_semaphore()
    targets = [sibling] + [d for _, d in group] + [d for _, d in far]
    for d in targets:
        pl.semaphore_signal(barrier, inc=1, device_id=d, device_id_type=mesh_id)

    for yy in range(2):
        for xx in range(n_x):
            g = yy * n_x + xx
            send_a[g, :, :a_rows, :] = a_ref[:, yy, xx, 1 - core].astype(BF16)
            send_a[g, :, a_rows:, :] = b_ref[:, yy, xx, 1 - core].astype(BF16)
    pl.semaphore_wait(barrier, len(targets))
    copies_a = []
    for o in range(n_group):
        g = lax.rem(own_g + 1 + o, n_group)
        copy = pltpu.make_async_remote_copy(
            src_ref=send_a.at[g],
            dst_ref=recv_a.at[g],
            send_sem=sem_a.at[0, g],
            recv_sem=sem_a.at[1, g],
            device_id=sibling,
            device_id_type=mesh_id,
        )
        copy.start()
        copies_a.append((g, copy))

    copies_b = []
    for o in range(n_group):
        g, copy = copies_a[o]
        copy.wait_recv()
        yy, xx = g // n_x, lax.rem(g, n_x)
        top = a_ref[:, yy, xx, core] + recv_a[g, :, :a_rows, :].astype(F32)
        low = b_ref[:, yy, xx, core] + recv_a[g, :, a_rows:, :].astype(F32)
        if o < n_group - 1:
            send_b[g, :, :a_rows, :] = top.astype(BF16)
            send_b[g, :, a_rows:, :] = low.astype(BF16)
            out = pltpu.make_async_remote_copy(
                src_ref=send_b.at[g],
                dst_ref=recv_b.at[own_g],
                send_sem=sem_b.at[0, g],
                recv_sem=sem_b.at[1, own_g],
                device_id=group[o][1],
                device_id_type=mesh_id,
            )
            out.start()
            copies_b.append(out)
        else:
            mid[:, :a_rows, :] = top
            mid[:, a_rows:, :] = low

    for g, d in group:
        pltpu.make_async_remote_copy(
            src_ref=send_b.at[g],
            dst_ref=recv_b.at[g],
            send_sem=sem_b.at[0, g],
            recv_sem=sem_b.at[1, g],
            device_id=d,
            device_id_type=mesh_id,
        ).wait_recv()
        mid[...] += recv_b[g].astype(F32)

    copies_c = []
    for t, d in far:
        send_c[t] = mid[t].astype(BF16)
        out = pltpu.make_async_remote_copy(
            src_ref=send_c.at[t],
            dst_ref=recv_c.at[z],
            send_sem=sem_c.at[0, t],
            recv_sem=sem_c.at[1, z],
            device_id=d,
            device_id_type=mesh_id,
        )
        out.start()
        copies_c.append(out)
    last[...] = mid[z]
    for t, d in far:
        pltpu.make_async_remote_copy(
            src_ref=send_c.at[t],
            dst_ref=recv_c.at[t],
            send_sem=sem_c.at[0, t],
            recv_sem=sem_c.at[1, t],
            device_id=d,
            device_id_type=mesh_id,
        ).wait_recv()
        last[...] += recv_c[t].astype(F32)
    a_out[...] = last[:a_rows, :] * factor
    b_out[...] = last[a_rows:, :] * factor
    for _, copy in copies_a:
        copy.wait_send()
    for copy in copies_b + copies_c:
        copy.wait_send()


def factor_sums(n_local, n_node, factor, a, b):
    n_x, n_z = n_local // 2, n_node // 2
    n_dev = n_local * n_node

    def lay(v):
        size = v.shape[0] // n_dev
        padded = -(-size // 16) * 16
        v = v.reshape(n_dev, size, v.shape[1])
        if padded != size:
            v = jnp.pad(v, ((0, 0), (0, padded - size), (0, 0)))
        return v.reshape(n_z, 2, n_x, 2, padded, v.shape[2]), size, padded

    a, a_size, a_rows = lay(a)
    b, b_size, b_rows = lay(b)
    rows = a_rows + b_rows
    wide = a.shape[-1]
    n_group = 2 * n_x
    vmem = pl.BlockSpec(memory_space=pltpu.VMEM)
    a_out, b_out = pl.pallas_call(
        functools.partial(sum_kernel, n_local, n_node, factor),
        out_shape=(
            jax.ShapeDtypeStruct((a_rows, wide), F32),
            jax.ShapeDtypeStruct((b_rows, wide), F32),
        ),
        in_specs=[vmem, vmem],
        out_specs=(vmem, vmem),
        scratch_shapes=[
            pltpu.VMEM((n_group, n_z, rows, wide), BF16),
            pltpu.VMEM((n_group, n_z, rows, wide), BF16),
            pltpu.VMEM((n_group, n_z, rows, wide), BF16),
            pltpu.VMEM((n_group, n_z, rows, wide), BF16),
            pltpu.VMEM((n_z, rows, wide), BF16),
            pltpu.VMEM((n_z, rows, wide), BF16),
            pltpu.VMEM((n_z, rows, wide), F32),
            pltpu.VMEM((rows, wide), F32),
            pltpu.SemaphoreType.DMA((2, n_group)),
            pltpu.SemaphoreType.DMA((2, n_group)),
            pltpu.SemaphoreType.DMA((2, n_z)),
        ],
        compiler_params=pltpu.CompilerParams(
            collective_id=1, has_side_effects=True, vmem_limit_bytes=48 * 2**20
        ),
        name="factor_sums",
    )(a, b)
    return a_out[:a_size], b_out[:b_size]


def hand_out_kernel(parts, c_in, a_in, b_in, c_out, a_out, b_out, sem):
    step = c_in.shape[0] // parts
    spans = [(c_in, c_out, i * step, step) for i in range(parts)]
    spans += [(a_in, a_out, 0, a_in.shape[0]), (b_in, b_out, 0, b_in.shape[0])]
    copies = [
        pltpu.make_async_copy(src.at[at : at + n], dst.at[at : at + n], sem.at[i])
        for i, (src, dst, at, n) in enumerate(spans)
    ]
    for copy in copies:
        copy.start()
    for copy in copies:
        copy.wait()


def hand_out(*arrays):
    parts = 4
    hbm = pl.BlockSpec(memory_space=pl.ANY)
    return pl.pallas_call(
        functools.partial(hand_out_kernel, parts),
        out_shape=tuple(jax.ShapeDtypeStruct(v.shape, v.dtype) for v in arrays),
        in_specs=[hbm] * 3,
        out_specs=(hbm,) * 3,
        scratch_shapes=[pltpu.SemaphoreType.DMA((parts + 2,))],
        compiler_params=pltpu.CompilerParams(vmem_limit_bytes=60 * 2**20),
        name="hand_out",
    )(*arrays)


def local(n_local, n_node, *args):
    activations, queries, rotated_key_value, attention_out_grad, adapter_down, adapter_up = args[:6]
    rows, width = activations.shape
    peers = n_local + n_node
    entries = peers * CHUNK
    vmem = pl.BlockSpec(memory_space=pltpu.VMEM)
    hbm = pl.BlockSpec(memory_space=pl.ANY)
    n_dev = n_local * n_node
    wide = 2 * ADAPTER_RANK
    factor = 1.0 / math.sqrt(rows * n_dev)
    a_rows, b_rows = width // n_dev, KEY_HEAD_WIDTH // n_dev
    fused = a_rows % 16 == 0 and b_rows % 16 == 0
    shrink = n_dev if fused else 1
    extra = []
    if fused:
        n_z, n_group, size = n_node // 2, n_local, a_rows + b_rows
        slab = (n_z, n_group, size, wide)
        extra = [
            pltpu.VMEM((KEY_HEAD_WIDTH, wide), F32),
            pltpu.VMEM(slab, BF16),
            pltpu.VMEM(slab, BF16),
            pltpu.VMEM(slab, BF16),
            pltpu.VMEM(slab, BF16),
            pltpu.VMEM((n_z, size, wide), BF16),
            pltpu.VMEM((n_z, size, wide), BF16),
            pltpu.VMEM((n_z, 2 * n_group, a_rows, wide), F32),
            pltpu.VMEM((n_z, size, wide), F32),
            pltpu.VMEM((size, wide), F32),
            pltpu.SemaphoreType.DMA((2, n_z)),
            pltpu.SemaphoreType.DMA((2, n_z, n_group)),
            pltpu.SemaphoreType.DMA((2, n_z)),
        ]
    cotangent, down_grad, up_grad = pl.pallas_call(
        functools.partial(main_kernel, n_local, n_node, factor if fused else None),
        out_shape=(
            jax.ShapeDtypeStruct((rows, 2 * KEY_HEAD_WIDTH), BF16),
            jax.ShapeDtypeStruct((width // shrink, wide), F32),
            jax.ShapeDtypeStruct((KEY_HEAD_WIDTH // shrink, wide), F32),
        ),
        in_specs=[hbm] * 12,
        out_specs=(hbm, vmem, vmem),
        scratch_shapes=[
            pltpu.VMEM((6, 1, rows), jnp.int32),
            pltpu.VMEM(adapter_up.shape, BF16),
            pltpu.VMEM((ROUNDS, rows, PAIR * GW), BF16),
            pltpu.VMEM((rows, width), BF16),
            pltpu.VMEM((width, rows), BF16),
            pltpu.VMEM((width, 2 * ADAPTER_RANK), BF16),
            pltpu.VMEM((rows, 2 * ADAPTER_RANK), BF16),
            pltpu.VMEM((ROUNDS, peers, CHUNK, GQ), BF16),
            pltpu.VMEM((peers, CHUNK, 2 * ADAPTER_RANK), BF16),
            pltpu.VMEM((peers, CHUNK, 2 * ADAPTER_RANK), BF16),
            pltpu.VMEM((ROUNDS, peers, CHUNK, GQ), BF16),
            pltpu.VMEM((peers, CHUNK, 2 * ADAPTER_RANK), BF16),
            pltpu.VMEM((peers, CHUNK, 2 * ADAPTER_RANK), BF16),
            pltpu.VMEM((4, entries, rows), BF16),
            pltpu.VMEM((rows, rows), BF16),
            pltpu.VMEM((4, rows, entries), BF16),
            pltpu.VMEM((rows, rows), F32),
            pltpu.VMEM((rows, HEAD), F32),
            pltpu.VMEM((rows, HEAD), F32),
            pltpu.VMEM((PAIR, rows // HEAD, GROUP * HEAD, HEAD), BF16),
            pltpu.VMEM((PAIR, rows // HEAD, GROUP * HEAD, HEAD), BF16),
            pltpu.VMEM((PAIR, 2, rows, HEAD), BF16),
            pltpu.VMEM((PAIR, rows // HEAD, rows, GROUP * HEAD), BF16),
            pltpu.VMEM((PAIR, rows // HEAD, rows, GROUP * HEAD), BF16),
            pltpu.VMEM((KV_HEADS, rows, HEAD), BF16),
            pltpu.VMEM((KV_HEADS, rows, HEAD), BF16),
            pltpu.VMEM((rows, 2 * ADAPTER_RANK), F32),
            pltpu.SemaphoreType.DMA((6,)),
            pltpu.SemaphoreType.DMA((ROUNDS, 4 * PAIR)),
            pltpu.SemaphoreType.DMA((3,)),
            pltpu.SemaphoreType.DMA((KV_HEADS, 2)),
            pltpu.SemaphoreType.DMA((ROUNDS + 2, peers)),
            pltpu.SemaphoreType.DMA((ROUNDS + 2, peers)),
            *extra,
        ],
        compiler_params=pltpu.CompilerParams(
            collective_id=0, has_side_effects=True, vmem_limit_bytes=60 * 2**20
        ),
        name="exchange_attention",
    )(*args)
    if fused:
        return hand_out(cotangent, down_grad, up_grad)
    down_sum, up_sum = factor_sums(n_local, n_node, factor, down_grad, up_grad)
    return cotangent, down_sum, up_sum


def solution(mesh):
    placed = (P(("node", "local"), None),) * 4 + (P(),) * 2 + (P(("node", "local"), None),) * 6
    return jax.shard_map(
        functools.partial(local, mesh.shape["local"], mesh.shape["node"]),
        mesh=mesh,
        in_specs=placed,
        out_specs=(P(("node", "local"), None),) * 3,
        check_vma=False,
    )
```

```python
import functools
import math

import jax
import jax.numpy as jnp
import numpy as np
from jax import lax
from jax.experimental import pallas as pl
from jax.experimental.pallas import tpu as pltpu
from jax.sharding import PartitionSpec as P

KV_HEADS = 8
HEAD = 128
ADAPTER_RANK = 64
CAP = 4
GROUP = 5
KEY_HEAD_WIDTH = 1024
CHUNK = 16
GW = (2 * GROUP + 2) * HEAD
PAIR = 2
ROUNDS = KV_HEADS // PAIR
GQ = PAIR * GW // 4
ROPE_THETA = 1000000.0
F32 = jnp.float32
BF16 = jnp.bfloat16


def dot(a, b):
    return jnp.dot(a, b, preferred_element_type=F32)


def dot_t(a, b):
    return lax.dot_general(a, b, (((1,), (1,)), ((), ())), preferred_element_type=F32)


def dot_l(a, b):
    return lax.dot_general(a, b, (((0,), (0,)), ((), ())), preferred_element_type=F32)


def iota(shape, axis):
    return lax.broadcasted_iota(jnp.int32, shape, axis)


def column(row):
    rows = row.shape[1]
    wide = jnp.broadcast_to(row.astype(F32), (128, rows))
    return jnp.transpose(wide)[:, 0:1].astype(jnp.int32)


def main_kernel(
    n_local,
    n_node,
    factor,
    x_hbm,
    q_hbm,
    kv_hbm,
    g_hbm,
    down_hbm,
    up_hbm,
    bl_hbm,
    bo_hbm,
    sn_hbm,
    so_hbm,
    pick_hbm,
    seg_hbm,
    cot_hbm,
    *rest,
):
    if factor is None:
        ddown_ref, dup_ref = rest[:2]
    else:
        down_sum, up_sum = rest[:2]
        dup_ref, send_a, recv_a, send_b, recv_b, send_c, recv_c = rest[-13:-6]
        own_part, mid, last, sem_a, sem_b, sem_c = rest[-6:]
    (
        ints,
        up_ref,
        stage,
        x_st,
        x_turned,
        down_v,
        down_rows,
        send,
        send_d,
        send_l,
        arr,
        arr_d,
        arr_l,
        pack_hot,
        slot_hot,
        bias,
        cos_v,
        sin_v,
        qs,
        gs,
        kvs,
        probs_s,
        grads_s,
        keys_out,
        vals_out,
        lift,
        int_sem,
        load_sem,
        xload_sem,
        out_sem,
        send_sem,
        recv_sem,
    ) = rest[2:34]
    rows = x_st.shape[0]
    width = x_st.shape[1]
    block = HEAD
    own_l = lax.axis_index("local")
    own_n = lax.axis_index("node")
    peers = n_local + n_node
    entries = peers * CHUNK

    def load(r):
        copies = []
        spans = []
        for u in range(PAIR):
            j, to = r * PAIR + u, u * GW
            spans += [
                (q_hbm, j * (GROUP * HEAD), GROUP * HEAD, to),
                (g_hbm, j * (GROUP * HEAD), GROUP * HEAD, to + GROUP * HEAD),
                (kv_hbm, j * HEAD, HEAD, to + 2 * GROUP * HEAD),
                (kv_hbm, KEY_HEAD_WIDTH + j * HEAD, HEAD, to + (2 * GROUP + 1) * HEAD),
            ]
        for i, (src, at, size, to) in enumerate(spans):
            copies.append(
                pltpu.make_async_copy(
                    src.at[:, pl.ds(pl.multiple_of(at, HEAD), size)],
                    stage.at[r, :, to : to + size],
                    load_sem.at[r, i],
                )
            )
        return copies

    x_copy = pltpu.make_async_copy(x_hbm, x_st, xload_sem.at[0])
    down_copy = pltpu.make_async_copy(down_hbm, down_v, xload_sem.at[1])
    up_copy = pltpu.make_async_copy(up_hbm, up_ref, xload_sem.at[2])
    int_copies = [
        pltpu.make_async_copy(src, ints.at[i], int_sem.at[i])
        for i, src in enumerate((bl_hbm, bo_hbm, sn_hbm, so_hbm, pick_hbm, seg_hbm))
    ]
    for copy in int_copies:
        copy.start()

    barrier = pltpu.get_barrier_semaphore()
    for o in range(1, n_local):
        pl.semaphore_signal(
            barrier,
            inc=1,
            device_id={"local": lax.rem(own_l + o, n_local)},
            device_id_type=pl.DeviceIdType.MESH,
        )
    for o in range(1, n_node):
        pl.semaphore_signal(
            barrier,
            inc=1,
            device_id={"node": lax.rem(own_n + o, n_node)},
            device_id_type=pl.DeviceIdType.MESH,
        )

    def start_load(j, c):
        for copy in load(j):
            copy.start()
        return c

    lax.fori_loop(0, 2, start_load, 0)
    for copy in int_copies:
        copy.wait()
    near_bin, near_off, far_bin, far_off = ints[0], ints[1], ints[2], ints[3]

    moved_in = near_bin != own_l
    moved_out = far_bin != own_n
    code = jnp.where(
        moved_in,
        near_bin * CAP + near_off,
        jnp.where(moved_out, (n_local + far_bin) * CAP + far_off, -1),
    )
    a_sub = iota((entries, rows), 0)
    hit = code == (a_sub >> 4) * CAP + (a_sub & 3)
    for c in range(4):
        pack_hot[:, c * rows : (c + 1) * rows] = jnp.where(hit & (((a_sub >> 2) & 3) == c), 1.0, 0.0).astype(BF16)

    for slot in (own_l, n_local + own_n):
        arr_d[slot] = jnp.zeros(arr_d.shape[1:], BF16)
        arr_l[slot] = jnp.zeros(arr_l.shape[1:], BF16)

    def clear(j, c):
        for slot in (own_l, n_local + own_n):
            arr[j, slot] = jnp.zeros(arr.shape[2:], BF16)
        return c

    lax.fori_loop(0, ROUNDS, clear, 0)

    sum_peers = []
    if factor is not None:
        core, lx = lax.rem(own_l, 2), own_l // 2
        y, z = lax.rem(own_n, 2), own_n // 2
        n_x, n_z = n_local // 2, n_node // 2
        n_group = 2 * n_x
        own_g = y * n_x + lx
        sibling = {"local": lx * 2 + (1 - core), "node": own_n}
        group = []
        for o in range(1, n_group):
            g = lax.rem(own_g + o, n_group)
            to = {"local": lax.rem(g, n_x) * 2 + core, "node": z * 2 + g // n_x}
            group.append((g, to))
        far = []
        for o in range(1, n_z):
            t = lax.rem(z + o, n_z)
            far.append((t, {"local": own_l, "node": t * 2 + y}))
        sum_peers = [sibling] + [to for _, to in group] + [to for _, to in far]
        for to in sum_peers:
            pl.semaphore_signal(barrier, inc=1, device_id=to, device_id_type=pl.DeviceIdType.MESH)

    pl.semaphore_wait(barrier, n_local - 1 + n_node - 1 + len(sum_peers))

    def message(j, axis, o, src, dst):
        count, me, base = (n_local, own_l, 0) if axis == "local" else (n_node, own_n, n_local)
        to = lax.rem(me + o, count)
        return pltpu.make_async_remote_copy(
            src_ref=src.at[base + to],
            dst_ref=dst.at[base + me],
            send_sem=send_sem.at[j, base + to],
            recv_sem=recv_sem.at[j, base + me],
            device_id={axis: to},
            device_id_type=pl.DeviceIdType.MESH,
        )

    def arrival(j, axis, o, src, dst):
        count, me, base = (n_local, own_l, 0) if axis == "local" else (n_node, own_n, n_local)
        frm = lax.rem(me + count - o, count)
        return pltpu.make_async_remote_copy(
            src_ref=src.at[base + frm],
            dst_ref=dst.at[base + frm],
            send_sem=send_sem.at[j, base + frm],
            recv_sem=recv_sem.at[j, base + frm],
            device_id={axis: frm},
            device_id_type=pl.DeviceIdType.MESH,
        )

    hops = [("node", o) for o in range(1, n_node)] + [("local", o) for o in range(1, n_local)]

    def pack(j, carry):
        for copy in load(j):
            copy.wait()

        @pl.when(j + 2 < ROUNDS)
        def _():
            start_load(j + 2, 0)

        @pl.when(j + 2 == ROUNDS)
        def _():
            x_copy.start()
            down_copy.start()
            up_copy.start()

        quarters = [stage[j, :, c * GQ : (c + 1) * GQ] for c in range(4)]
        total = dot(pack_hot[...], jnp.concatenate(quarters, axis=0))
        send[j] = total.astype(BF16).reshape(peers, CHUNK, GQ)
        for axis, o in hops:
            message(j, axis, o, send.at[j], arr.at[j]).start()
        return carry

    lax.fori_loop(0, ROUNDS, pack, 0)

    pick = column(ints[4])
    own_picks = jnp.where(pick == iota((rows, rows), 1), 1.0, 0.0).astype(BF16)
    a_lane = iota((rows, entries), 1)
    got = pick == rows + (a_lane >> 4) * CAP + (a_lane & 3)
    for c in range(4):
        slot_hot[c, :, :rows] = own_picks
        slot_hot[c, :, rows:] = jnp.where(got & (((a_lane >> 2) & 3) == c), 1.0, 0.0).astype(BF16)

    x_copy.wait()
    down_copy.wait()
    down_rows[...] = dot(x_st[...], down_v[...]).astype(BF16)
    send_d[...] = dot(pack_hot[:, :rows], down_rows[...]).astype(BF16).reshape(send_d.shape)
    for axis, o in hops:
        message(ROUNDS, axis, o, send_d, arr_d).start()

    seg_row = ints[5]
    seg_col = column(seg_row)
    allowed = (seg_col == seg_row) & (iota((rows, rows), 0) <= iota((rows, rows), 1))
    bias[...] = jnp.where(allowed, 0.0, -1e30)
    first = jnp.sum(jnp.where(seg_row < seg_col, 1.0, 0.0), axis=1, keepdims=True)
    position = iota((rows, HEAD), 0).astype(F32) - first
    lane = iota((rows, HEAD), 1)
    half = lane % (HEAD // 2)
    frequency = jnp.exp(half.astype(F32) * (-2.0 * math.log(ROPE_THETA) / HEAD))
    angles = position * frequency
    cos_v[...] = jnp.cos(angles)
    sin_v[...] = jnp.where(lane < HEAD // 2, jnp.sin(angles), -jnp.sin(angles))
    lift[...] = jnp.zeros_like(lift)

    def turn(i, carry):
        at = pl.multiple_of(i * HEAD, HEAD)
        x_turned[pl.ds(at, HEAD), :] = jnp.transpose(x_st[:, pl.ds(at, HEAD)])
        return carry

    lax.fori_loop(0, width // HEAD, turn, 0)
    up_copy.wait()

    def remote(src, dst, to_sem, from_sem, to):
        return pltpu.make_async_remote_copy(
            src_ref=src,
            dst_ref=dst,
            send_sem=to_sem,
            recv_sem=from_sem,
            device_id=to,
            device_id_type=pl.DeviceIdType.MESH,
        )

    def sums(own_lift):
        a_rows, b_rows = down_sum.shape[0], up_sum.shape[0]

        slab_rows = 2 * n_group * a_rows

        def up_piece(t, g, at_core):
            part = (t * 2 + g // n_x) * n_local + lax.rem(g, n_x) * 2 + at_core
            return dup_ref[pl.ds(pl.multiple_of(part * b_rows, 16), b_rows), :]

        order = [t for t, _ in far] + [z]
        copies = []
        for t in order:
            slab = dot(x_turned[pl.ds(pl.multiple_of(t * slab_rows, 16), slab_rows), :], own_lift)
            own_part[t] = slab.reshape(2 * n_group, a_rows, slab.shape[1])
            for g in range(n_group):
                send_a[t, g, :a_rows, :] = own_part[t, g * 2 + 1 - core].astype(BF16)
                send_a[t, g, a_rows:, :] = up_piece(t, g, 1 - core).astype(BF16)
            copy = remote(send_a.at[t], recv_a.at[t], sem_a.at[0, t], sem_a.at[1, t], sibling)
            copy.start()
            copies.append(copy)
        for t, copy in zip(order, copies[:]):
            copy.wait_recv()
            for g, to in group:
                got = recv_a[t, g].astype(F32)
                a = own_part[t, g * 2 + core] + got[:a_rows]
                b = up_piece(t, g, core) + got[a_rows:]
                send_b[t, g, :a_rows, :] = a.astype(BF16)
                send_b[t, g, a_rows:, :] = b.astype(BF16)
                out = remote(
                    send_b.at[t, g],
                    recv_b.at[t, own_g],
                    sem_b.at[0, t, g],
                    sem_b.at[1, t, own_g],
                    to,
                )
                out.start()
                copies.append(out)
            got = recv_a[t, own_g].astype(F32)
            mid[t, :a_rows, :] = own_part[t, own_g * 2 + core] + got[:a_rows]
            mid[t, a_rows:, :] = up_piece(t, own_g, core) + got[a_rows:]
        for i, t in enumerate(order):
            total = mid[t]
            for g, to in group:
                remote(
                    send_b.at[t, g], recv_b.at[t, g], sem_b.at[0, t, g], sem_b.at[1, t, g], to
                ).wait_recv()
                total += recv_b[t, g].astype(F32)
            if i < len(far):
                send_c[t] = total.astype(BF16)
                out = remote(
                    send_c.at[t], recv_c.at[z], sem_c.at[0, t], sem_c.at[1, z], far[i][1]
                )
                out.start()
                copies.append(out)
            else:
                last[...] = total
        for t, to in far:
            remote(
                send_c.at[t], recv_c.at[t], sem_c.at[0, t], sem_c.at[1, t], to
            ).wait_recv()
            last[...] += recv_c[t].astype(F32)
        down_sum[...] = last[:a_rows, :] * factor
        up_sum[...] = last[a_rows:, :] * factor
        for copy in copies:
            copy.wait_send()

    scale = 1.0 / math.sqrt(HEAD)
    exp_scale = scale * math.log2(math.e)
    up_row = iota((2 * ADAPTER_RANK, HEAD), 0)

    def cot_copies(j):
        return (
            pltpu.make_async_copy(
                keys_out.at[j],
                cot_hbm.at[:, pl.ds(pl.multiple_of(j * HEAD, HEAD), HEAD)],
                out_sem.at[j, 0],
            ),
            pltpu.make_async_copy(
                vals_out.at[j],
                cot_hbm.at[:, pl.ds(pl.multiple_of(KEY_HEAD_WIDTH + j * HEAD, HEAD), HEAD)],
                out_sem.at[j, 1],
            ),
        )

    def head(r, carry):
        for axis, o in hops:
            arrival(r, axis, o, send.at[r], arr.at[r]).wait_recv()
        arrived = arr[r].reshape(entries, GQ)
        per = GQ // HEAD
        for c in range(4):
            listed = jnp.concatenate([stage[r, :, c * GQ : (c + 1) * GQ], arrived], axis=0)
            part = dot(slot_hot[c], listed).astype(BF16)
            for i in range(per):
                u, col = divmod(c * per + i, 2 * GROUP + 2)
                piece = part[:, i * HEAD : (i + 1) * HEAD]
                if col >= 2 * GROUP:
                    kvs[u, col - 2 * GROUP] = piece
                    continue
                dst, h = (qs, col) if col < GROUP else (gs, col - GROUP)
                for b in range(rows // block):
                    dst[u, b, h * block : (h + 1) * block, :] = piece[b * block : (b + 1) * block]
        tasks = [(u, b) for b in range(rows // block) for u in range(PAIR)]
        d_keys = [[jnp.zeros((block, HEAD), F32)] * (rows // block) for _ in range(PAIR)]
        d_vals = [[jnp.zeros((block, HEAD), F32)] * (rows // block) for _ in range(PAIR)]

        def products(u, b):
            seen = (b + 1) * block
            return dot_t(kvs[u, 0, :seen, :], qs[u, b]), dot_t(kvs[u, 1, :seen, :], gs[u, b])

        ahead = products(*tasks[0])
        for i, (u, b) in enumerate(tasks):
            scores, prob_grads = ahead
            if i + 1 < len(tasks):
                ahead = products(*tasks[i + 1])
            seen = (b + 1) * block
            mask = bias[:seen, b * block : (b + 1) * block]
            for h in range(GROUP):
                cols = slice(h * block, (h + 1) * block)
                score = scores[:, cols] + mask
                top = jnp.max(score, axis=0, keepdims=True)
                weights = jnp.exp2((score - top) * exp_scale)
                probs = weights * (1.0 / jnp.sum(weights, axis=0, keepdims=True))
                prob_grad = prob_grads[:, cols]
                delta = jnp.sum(probs * prob_grad, axis=0, keepdims=True)
                probs_s[u, b, :seen, cols] = probs.astype(BF16)
                grads_s[u, b, :seen, cols] = (probs * (prob_grad - delta)).astype(BF16)
            d_val = dot(probs_s[u, b, :seen, :], gs[u, b])
            d_key = dot(grads_s[u, b, :seen, :], qs[u, b])
            for t in range(b + 1):
                d_vals[u][t] += d_val[t * block : (t + 1) * block]
                d_keys[u][t] += d_key[t * block : (t + 1) * block]
        total = lift[...]
        for u in range(PAIR):
            j = r * PAIR + u
            d_key = jnp.concatenate(d_keys[u], axis=0) * scale
            d_key = d_key * cos_v[...] + pltpu.roll(d_key, HEAD // 2, 1) * sin_v[...]
            key_low = d_key.astype(BF16)
            val_low = jnp.concatenate(d_vals[u], axis=0).astype(BF16)
            keys_out[j] = key_low
            vals_out[j] = val_low
            up = up_ref[:, pl.ds(pl.multiple_of(j * HEAD, HEAD), HEAD)].astype(F32)
            up_key = jnp.where(up_row < ADAPTER_RANK, up, 0.0).astype(BF16)
            up_val = jnp.where(up_row < ADAPTER_RANK, 0.0, up).astype(BF16)
            total += dot_t(key_low, up_key) + dot_t(val_low, up_val)
        lift[...] = total
        for u in range(PAIR):
            for copy in cot_copies(r * PAIR + u):
                copy.start()
        return carry

    lax.fori_loop(0, ROUNDS, head, 0)

    lift_low = lift[...].astype(BF16)
    send_l[...] = dot_l(slot_hot[0, :, rows:], lift_low).astype(BF16).reshape(send_l.shape)
    for axis, o in hops:
        message(ROUNDS + 1, axis, o, send_l, arr_l).start()

    for axis, o in hops:
        arrival(ROUNDS, axis, o, send_d, arr_d).wait_recv()
    down_out = dot(slot_hot[0, :, :rows], down_rows[...])
    down_out += dot(slot_hot[0, :, rows:], arr_d[...].reshape(entries, HEAD))
    down_low = down_out.astype(BF16)
    down_lane = iota((HEAD, 2 * ADAPTER_RANK), 1) < ADAPTER_RANK

    def up_grad(j, carry):
        from_key = dot_l(keys_out[j], down_low)
        from_val = dot_l(vals_out[j], down_low)
        dup_ref[pl.ds(pl.multiple_of(j * HEAD, HEAD), HEAD), :] = jnp.where(
            down_lane, from_key, from_val
        )
        return carry

    lax.fori_loop(0, KV_HEADS, up_grad, 0)

    own_lift = dot_l(slot_hot[0, :, :rows], lift_low)
    for axis, o in hops:
        arrival(ROUNDS + 1, axis, o, send_l, arr_l).wait_recv()
    own_lift += dot_l(pack_hot[:, :rows], arr_l[...].reshape(entries, HEAD))
    own_lift = own_lift.astype(BF16)
    if factor is None:
        span = width // 8
        for c in range(8):
            at = slice(c * span, (c + 1) * span)
            ddown_ref[at, :] = dot(x_turned[at, :], own_lift)
    else:
        sums(own_lift)

    def finish(j, carry):
        for copy in cot_copies(j):
            copy.wait()
        return carry

    lax.fori_loop(0, KV_HEADS, finish, 0)

    def sent(r, carry):
        for axis, o in hops:
            message(r, axis, o, send.at[r], arr.at[r]).wait_send()
        return carry

    lax.fori_loop(0, ROUNDS, sent, 0)
    for axis, o in hops:
        message(ROUNDS, axis, o, send_d, arr_d).wait_send()
        message(ROUNDS + 1, axis, o, send_l, arr_l).wait_send()


def sum_kernel(
    n_local,
    n_node,
    factor,
    a_ref,
    b_ref,
    a_out,
    b_out,
    send_a,
    recv_a,
    send_b,
    recv_b,
    send_c,
    recv_c,
    mid,
    last,
    sem_a,
    sem_b,
    sem_c,
):
    n_x, n_z = n_local // 2, n_node // 2
    own_l = lax.axis_index("local")
    own_n = lax.axis_index("node")
    core, lx = lax.rem(own_l, 2), own_l // 2
    y, z = lax.rem(own_n, 2), own_n // 2
    a_rows = a_ref.shape[4]
    n_group = 2 * n_x
    own_g = y * n_x + lx
    mesh_id = pl.DeviceIdType.MESH

    sibling = {"local": lx * 2 + (1 - core), "node": own_n}
    group = []
    for o in range(1, n_group):
        g = lax.rem(own_g + o, n_group)
        group.append((g, {"local": lax.rem(g, n_x) * 2 + core, "node": z * 2 + g // n_x}))
    far = []
    for o in range(1, n_z):
        t = lax.rem(z + o, n_z)
        far.append((t, {"local": own_l, "node": t * 2 + y}))

    barrier = pltpu.get_barrier_semaphore()
    targets = [sibling] + [d for _, d in group] + [d for _, d in far]
    for d in targets:
        pl.semaphore_signal(barrier, inc=1, device_id=d, device_id_type=mesh_id)

    for yy in range(2):
        for xx in range(n_x):
            g = yy * n_x + xx
            send_a[g, :, :a_rows, :] = a_ref[:, yy, xx, 1 - core].astype(BF16)
            send_a[g, :, a_rows:, :] = b_ref[:, yy, xx, 1 - core].astype(BF16)
    pl.semaphore_wait(barrier, len(targets))
    copies_a = []
    for o in range(n_group):
        g = lax.rem(own_g + 1 + o, n_group)
        copy = pltpu.make_async_remote_copy(
            src_ref=send_a.at[g],
            dst_ref=recv_a.at[g],
            send_sem=sem_a.at[0, g],
            recv_sem=sem_a.at[1, g],
            device_id=sibling,
            device_id_type=mesh_id,
        )
        copy.start()
        copies_a.append((g, copy))

    copies_b = []
    for o in range(n_group):
        g, copy = copies_a[o]
        copy.wait_recv()
        yy, xx = g // n_x, lax.rem(g, n_x)
        top = a_ref[:, yy, xx, core] + recv_a[g, :, :a_rows, :].astype(F32)
        low = b_ref[:, yy, xx, core] + recv_a[g, :, a_rows:, :].astype(F32)
        if o < n_group - 1:
            send_b[g, :, :a_rows, :] = top.astype(BF16)
            send_b[g, :, a_rows:, :] = low.astype(BF16)
            out = pltpu.make_async_remote_copy(
                src_ref=send_b.at[g],
                dst_ref=recv_b.at[own_g],
                send_sem=sem_b.at[0, g],
                recv_sem=sem_b.at[1, own_g],
                device_id=group[o][1],
                device_id_type=mesh_id,
            )
            out.start()
            copies_b.append(out)
        else:
            mid[:, :a_rows, :] = top
            mid[:, a_rows:, :] = low

    for g, d in group:
        pltpu.make_async_remote_copy(
            src_ref=send_b.at[g],
            dst_ref=recv_b.at[g],
            send_sem=sem_b.at[0, g],
            recv_sem=sem_b.at[1, g],
            device_id=d,
            device_id_type=mesh_id,
        ).wait_recv()
        mid[...] += recv_b[g].astype(F32)

    copies_c = []
    for t, d in far:
        send_c[t] = mid[t].astype(BF16)
        out = pltpu.make_async_remote_copy(
            src_ref=send_c.at[t],
            dst_ref=recv_c.at[z],
            send_sem=sem_c.at[0, t],
            recv_sem=sem_c.at[1, z],
            device_id=d,
            device_id_type=mesh_id,
        )
        out.start()
        copies_c.append(out)
    last[...] = mid[z]
    for t, d in far:
        pltpu.make_async_remote_copy(
            src_ref=send_c.at[t],
            dst_ref=recv_c.at[t],
            send_sem=sem_c.at[0, t],
            recv_sem=sem_c.at[1, t],
            device_id=d,
            device_id_type=mesh_id,
        ).wait_recv()
        last[...] += recv_c[t].astype(F32)
    a_out[...] = last[:a_rows, :] * factor
    b_out[...] = last[a_rows:, :] * factor
    for _, copy in copies_a:
        copy.wait_send()
    for copy in copies_b + copies_c:
        copy.wait_send()


def factor_sums(n_local, n_node, factor, a, b):
    n_x, n_z = n_local // 2, n_node // 2
    n_dev = n_local * n_node

    def lay(v):
        size = v.shape[0] // n_dev
        padded = -(-size // 16) * 16
        v = v.reshape(n_dev, size, v.shape[1])
        if padded != size:
            v = jnp.pad(v, ((0, 0), (0, padded - size), (0, 0)))
        return v.reshape(n_z, 2, n_x, 2, padded, v.shape[2]), size, padded

    a, a_size, a_rows = lay(a)
    b, b_size, b_rows = lay(b)
    rows = a_rows + b_rows
    wide = a.shape[-1]
    n_group = 2 * n_x
    vmem = pl.BlockSpec(memory_space=pltpu.VMEM)
    a_out, b_out = pl.pallas_call(
        functools.partial(sum_kernel, n_local, n_node, factor),
        out_shape=(
            jax.ShapeDtypeStruct((a_rows, wide), F32),
            jax.ShapeDtypeStruct((b_rows, wide), F32),
        ),
        in_specs=[vmem, vmem],
        out_specs=(vmem, vmem),
        scratch_shapes=[
            pltpu.VMEM((n_group, n_z, rows, wide), BF16),
            pltpu.VMEM((n_group, n_z, rows, wide), BF16),
            pltpu.VMEM((n_group, n_z, rows, wide), BF16),
            pltpu.VMEM((n_group, n_z, rows, wide), BF16),
            pltpu.VMEM((n_z, rows, wide), BF16),
            pltpu.VMEM((n_z, rows, wide), BF16),
            pltpu.VMEM((n_z, rows, wide), F32),
            pltpu.VMEM((rows, wide), F32),
            pltpu.SemaphoreType.DMA((2, n_group)),
            pltpu.SemaphoreType.DMA((2, n_group)),
            pltpu.SemaphoreType.DMA((2, n_z)),
        ],
        compiler_params=pltpu.CompilerParams(
            collective_id=1, has_side_effects=True, vmem_limit_bytes=48 * 2**20
        ),
        name="factor_sums",
    )(a, b)
    return a_out[:a_size], b_out[:b_size]


def hand_out_kernel(parts, c_in, a_in, b_in, c_out, a_out, b_out, c_v, a_v, b_v, sem):
    step = c_in.shape[0] // parts
    spans = [(c_in, c_v, c_out, i * step, step) for i in range(parts)]
    spans += [(a_in, a_v, a_out, 0, a_in.shape[0]), (b_in, b_v, b_out, 0, b_in.shape[0])]
    loads, stores = [], []
    for i, (src, mid, dst, at, n) in enumerate(spans):
        rows = slice(at, at + n)
        loads.append(pltpu.make_async_copy(src.at[rows], mid.at[rows], sem.at[0, i]))
        stores.append(pltpu.make_async_copy(mid.at[rows], dst.at[rows], sem.at[1, i]))
    for copy in loads:
        copy.start()
    for first, second in zip(loads, stores):
        first.wait()
        second.start()
    for copy in stores:
        copy.wait()


def hand_out(*arrays):
    parts = 4
    hbm = pl.BlockSpec(memory_space=pl.ANY)
    return pl.pallas_call(
        functools.partial(hand_out_kernel, parts),
        out_shape=tuple(jax.ShapeDtypeStruct(v.shape, v.dtype) for v in arrays),
        in_specs=[hbm] * 3,
        out_specs=(hbm,) * 3,
        scratch_shapes=[pltpu.VMEM(v.shape, v.dtype) for v in arrays]
        + [pltpu.SemaphoreType.DMA((2, parts + 2))],
        compiler_params=pltpu.CompilerParams(vmem_limit_bytes=60 * 2**20),
        name="hand_out",
    )(*arrays)


def local(n_local, n_node, *args):
    activations, queries, rotated_key_value, attention_out_grad, adapter_down, adapter_up = args[:6]
    rows, width = activations.shape
    peers = n_local + n_node
    entries = peers * CHUNK
    vmem = pl.BlockSpec(memory_space=pltpu.VMEM)
    hbm = pl.BlockSpec(memory_space=pl.ANY)
    n_dev = n_local * n_node
    wide = 2 * ADAPTER_RANK
    factor = 1.0 / math.sqrt(rows * n_dev)
    a_rows, b_rows = width // n_dev, KEY_HEAD_WIDTH // n_dev
    fused = a_rows % 16 == 0 and b_rows % 16 == 0
    shrink = n_dev if fused else 1
    extra = []
    if fused:
        n_z, n_group, size = n_node // 2, n_local, a_rows + b_rows
        slab = (n_z, n_group, size, wide)
        extra = [
            pltpu.VMEM((KEY_HEAD_WIDTH, wide), F32),
            pltpu.VMEM(slab, BF16),
            pltpu.VMEM(slab, BF16),
            pltpu.VMEM(slab, BF16),
            pltpu.VMEM(slab, BF16),
            pltpu.VMEM((n_z, size, wide), BF16),
            pltpu.VMEM((n_z, size, wide), BF16),
            pltpu.VMEM((n_z, 2 * n_group, a_rows, wide), F32),
            pltpu.VMEM((n_z, size, wide), F32),
            pltpu.VMEM((size, wide), F32),
            pltpu.SemaphoreType.DMA((2, n_z)),
            pltpu.SemaphoreType.DMA((2, n_z, n_group)),
            pltpu.SemaphoreType.DMA((2, n_z)),
        ]
    cotangent, down_grad, up_grad = pl.pallas_call(
        functools.partial(main_kernel, n_local, n_node, factor if fused else None),
        out_shape=(
            jax.ShapeDtypeStruct((rows, 2 * KEY_HEAD_WIDTH), BF16),
            jax.ShapeDtypeStruct((width // shrink, wide), F32),
            jax.ShapeDtypeStruct((KEY_HEAD_WIDTH // shrink, wide), F32),
        ),
        in_specs=[hbm] * 12,
        out_specs=(hbm, vmem, vmem),
        scratch_shapes=[
            pltpu.VMEM((6, 1, rows), jnp.int32),
            pltpu.VMEM(adapter_up.shape, BF16),
            pltpu.VMEM((ROUNDS, rows, PAIR * GW), BF16),
            pltpu.VMEM((rows, width), BF16),
            pltpu.VMEM((width, rows), BF16),
            pltpu.VMEM((width, 2 * ADAPTER_RANK), BF16),
            pltpu.VMEM((rows, 2 * ADAPTER_RANK), BF16),
            pltpu.VMEM((ROUNDS, peers, CHUNK, GQ), BF16),
            pltpu.VMEM((peers, CHUNK, 2 * ADAPTER_RANK), BF16),
            pltpu.VMEM((peers, CHUNK, 2 * ADAPTER_RANK), BF16),
            pltpu.VMEM((ROUNDS, peers, CHUNK, GQ), BF16),
            pltpu.VMEM((peers, CHUNK, 2 * ADAPTER_RANK), BF16),
            pltpu.VMEM((peers, CHUNK, 2 * ADAPTER_RANK), BF16),
            pltpu.VMEM((entries, 4 * rows), BF16),
            pltpu.VMEM((4, rows, rows + entries), BF16),
            pltpu.VMEM((rows, rows), F32),
            pltpu.VMEM((rows, HEAD), F32),
            pltpu.VMEM((rows, HEAD), F32),
            pltpu.VMEM((PAIR, rows // HEAD, GROUP * HEAD, HEAD), BF16),
            pltpu.VMEM((PAIR, rows // HEAD, GROUP * HEAD, HEAD), BF16),
            pltpu.VMEM((PAIR, 2, rows, HEAD), BF16),
            pltpu.VMEM((PAIR, rows // HEAD, rows, GROUP * HEAD), BF16),
            pltpu.VMEM((PAIR, rows // HEAD, rows, GROUP * HEAD), BF16),
            pltpu.VMEM((KV_HEADS, rows, HEAD), BF16),
            pltpu.VMEM((KV_HEADS, rows, HEAD), BF16),
            pltpu.VMEM((rows, 2 * ADAPTER_RANK), F32),
            pltpu.SemaphoreType.DMA((6,)),
            pltpu.SemaphoreType.DMA((ROUNDS, 4 * PAIR)),
            pltpu.SemaphoreType.DMA((3,)),
            pltpu.SemaphoreType.DMA((KV_HEADS, 2)),
            pltpu.SemaphoreType.DMA((ROUNDS + 2, peers)),
            pltpu.SemaphoreType.DMA((ROUNDS + 2, peers)),
            *extra,
        ],
        compiler_params=pltpu.CompilerParams(
            collective_id=0, has_side_effects=True, vmem_limit_bytes=60 * 2**20
        ),
        name="exchange_attention",
    )(*args)
    if fused:
        return hand_out(cotangent, down_grad, up_grad)
    down_sum, up_sum = factor_sums(n_local, n_node, factor, down_grad, up_grad)
    return cotangent, down_sum, up_sum


def solution(mesh):
    placed = (P(("node", "local"), None),) * 4 + (P(),) * 2 + (P(("node", "local"), None),) * 6
    return jax.shard_map(
        functools.partial(local, mesh.shape["local"], mesh.shape["node"]),
        mesh=mesh,
        in_specs=placed,
        out_specs=(P(("node", "local"), None),) * 3,
        check_vma=False,
    )
```

```python
import functools
import math

import jax
import jax.numpy as jnp
import numpy as np
from jax import lax
from jax.experimental import pallas as pl
from jax.experimental.pallas import tpu as pltpu
from jax.sharding import PartitionSpec as P

KV_HEADS = 8
HEAD = 128
ADAPTER_RANK = 64
CAP = 4
GROUP = 5
KEY_HEAD_WIDTH = 1024
CHUNK = 16
GW = (2 * GROUP + 2) * HEAD
PAIR = 2
ROUNDS = KV_HEADS // PAIR
GQ = PAIR * GW // 4
ROPE_THETA = 1000000.0
F32 = jnp.float32
BF16 = jnp.bfloat16


def dot(a, b):
    return jnp.dot(a, b, preferred_element_type=F32)


def dot_t(a, b):
    return lax.dot_general(a, b, (((1,), (1,)), ((), ())), preferred_element_type=F32)


def dot_l(a, b):
    return lax.dot_general(a, b, (((0,), (0,)), ((), ())), preferred_element_type=F32)


def iota(shape, axis):
    return lax.broadcasted_iota(jnp.int32, shape, axis)


def column(row):
    rows = row.shape[1]
    wide = jnp.broadcast_to(row.astype(F32), (128, rows))
    return jnp.transpose(wide)[:, 0:1].astype(jnp.int32)


def main_kernel(
    n_local,
    n_node,
    factor,
    x_hbm,
    q_hbm,
    kv_hbm,
    g_hbm,
    down_hbm,
    up_hbm,
    bl_hbm,
    bo_hbm,
    sn_hbm,
    so_hbm,
    pick_hbm,
    seg_hbm,
    cot_hbm,
    *rest,
):
    if factor is None:
        ddown_ref, dup_ref = rest[:2]
    else:
        down_sum, up_sum = rest[:2]
        dup_ref, send_a, recv_a, send_b, recv_b, send_c, recv_c = rest[-13:-6]
        own_part, mid, last, sem_a, sem_b, sem_c = rest[-6:]
    (
        ints,
        up_ref,
        stage,
        x_st,
        x_turned,
        down_v,
        down_rows,
        send,
        send_d,
        send_l,
        arr,
        arr_d,
        arr_l,
        pack_hot,
        slot_hot,
        bias,
        cos_v,
        sin_v,
        qs,
        gs,
        kvs,
        probs_s,
        grads_s,
        keys_out,
        vals_out,
        lift,
        int_sem,
        load_sem,
        xload_sem,
        out_sem,
        send_sem,
        recv_sem,
    ) = rest[2:34]
    rows = x_st.shape[0]
    width = x_st.shape[1]
    block = HEAD
    own_l = lax.axis_index("local")
    own_n = lax.axis_index("node")
    peers = n_local + n_node
    entries = peers * CHUNK

    def load(r):
        copies = []
        spans = []
        for u in range(PAIR):
            j, to = r * PAIR + u, u * GW
            spans += [
                (q_hbm, j * (GROUP * HEAD), GROUP * HEAD, to),
                (g_hbm, j * (GROUP * HEAD), GROUP * HEAD, to + GROUP * HEAD),
                (kv_hbm, j * HEAD, HEAD, to + 2 * GROUP * HEAD),
                (kv_hbm, KEY_HEAD_WIDTH + j * HEAD, HEAD, to + (2 * GROUP + 1) * HEAD),
            ]
        for i, (src, at, size, to) in enumerate(spans):
            copies.append(
                pltpu.make_async_copy(
                    src.at[:, pl.ds(pl.multiple_of(at, HEAD), size)],
                    stage.at[r, :, to : to + size],
                    load_sem.at[r, i],
                )
            )
        return copies

    x_copy = pltpu.make_async_copy(x_hbm, x_st, xload_sem.at[0])
    down_copy = pltpu.make_async_copy(down_hbm, down_v, xload_sem.at[1])
    up_copy = pltpu.make_async_copy(up_hbm, up_ref, xload_sem.at[2])
    int_copies = [
        pltpu.make_async_copy(src, ints.at[i], int_sem.at[i])
        for i, src in enumerate((bl_hbm, bo_hbm, sn_hbm, so_hbm, pick_hbm, seg_hbm))
    ]
    for copy in int_copies:
        copy.start()

    barrier = pltpu.get_barrier_semaphore()
    for o in range(1, n_local):
        pl.semaphore_signal(
            barrier,
            inc=1,
            device_id={"local": lax.rem(own_l + o, n_local)},
            device_id_type=pl.DeviceIdType.MESH,
        )
    for o in range(1, n_node):
        pl.semaphore_signal(
            barrier,
            inc=1,
            device_id={"node": lax.rem(own_n + o, n_node)},
            device_id_type=pl.DeviceIdType.MESH,
        )

    def start_load(j, c):
        for copy in load(j):
            copy.start()
        return c

    lax.fori_loop(0, 2, start_load, 0)
    for copy in int_copies:
        copy.wait()
    near_bin, near_off, far_bin, far_off = ints[0], ints[1], ints[2], ints[3]

    moved_in = near_bin != own_l
    moved_out = far_bin != own_n
    code = jnp.where(
        moved_in,
        near_bin * CAP + near_off,
        jnp.where(moved_out, (n_local + far_bin) * CAP + far_off, -1),
    )
    a_sub = iota((entries, rows), 0)
    hit = code == (a_sub >> 4) * CAP + (a_sub & 3)
    for c in range(4):
        pack_hot[:, c * rows : (c + 1) * rows] = jnp.where(hit & (((a_sub >> 2) & 3) == c), 1.0, 0.0).astype(BF16)

    for slot in (own_l, n_local + own_n):
        arr_d[slot] = jnp.zeros(arr_d.shape[1:], BF16)
        arr_l[slot] = jnp.zeros(arr_l.shape[1:], BF16)

    def clear(j, c):
        for slot in (own_l, n_local + own_n):
            arr[j, slot] = jnp.zeros(arr.shape[2:], BF16)
        return c

    lax.fori_loop(0, ROUNDS, clear, 0)

    sum_peers = []
    if factor is not None:
        core, lx = lax.rem(own_l, 2), own_l // 2
        y, z = lax.rem(own_n, 2), own_n // 2
        n_x, n_z = n_local // 2, n_node // 2
        n_group = 2 * n_x
        own_g = y * n_x + lx
        sibling = {"local": lx * 2 + (1 - core), "node": own_n}
        group = []
        for o in range(1, n_group):
            g = lax.rem(own_g + o, n_group)
            to = {"local": lax.rem(g, n_x) * 2 + core, "node": z * 2 + g // n_x}
            group.append((g, to))
        far = []
        for o in range(1, n_z):
            t = lax.rem(z + o, n_z)
            far.append((t, {"local": own_l, "node": t * 2 + y}))
        sum_peers = [sibling] + [to for _, to in group] + [to for _, to in far]
        for to in sum_peers:
            pl.semaphore_signal(barrier, inc=1, device_id=to, device_id_type=pl.DeviceIdType.MESH)

    pl.semaphore_wait(barrier, n_local - 1 + n_node - 1 + len(sum_peers))

    def message(j, axis, o, src, dst):
        count, me, base = (n_local, own_l, 0) if axis == "local" else (n_node, own_n, n_local)
        to = lax.rem(me + o, count)
        return pltpu.make_async_remote_copy(
            src_ref=src.at[base + to],
            dst_ref=dst.at[base + me],
            send_sem=send_sem.at[j, base + to],
            recv_sem=recv_sem.at[j, base + me],
            device_id={axis: to},
            device_id_type=pl.DeviceIdType.MESH,
        )

    def arrival(j, axis, o, src, dst):
        count, me, base = (n_local, own_l, 0) if axis == "local" else (n_node, own_n, n_local)
        frm = lax.rem(me + count - o, count)
        return pltpu.make_async_remote_copy(
            src_ref=src.at[base + frm],
            dst_ref=dst.at[base + frm],
            send_sem=send_sem.at[j, base + frm],
            recv_sem=recv_sem.at[j, base + frm],
            device_id={axis: frm},
            device_id_type=pl.DeviceIdType.MESH,
        )

    hops = [("node", o) for o in range(1, n_node)] + [("local", o) for o in range(1, n_local)]

    def send_round(j):
        for axis, o in hops:
            message(j, axis, o, send.at[j], arr.at[j]).start()

    def pack(j, carry):
        for copy in load(j):
            copy.wait()

        @pl.when(j + 2 < ROUNDS)
        def _():
            start_load(j + 2, 0)

        @pl.when(j + 2 == ROUNDS)
        def _():
            x_copy.start()
            down_copy.start()
            up_copy.start()

        quarters = [stage[j, :, c * GQ : (c + 1) * GQ] for c in range(4)]
        total = dot(pack_hot[...], jnp.concatenate(quarters, axis=0))
        send[j] = total.astype(BF16).reshape(peers, CHUNK, GQ)

        @pl.when(j < 2)
        def _():
            send_round(j)

        return carry

    lax.fori_loop(0, ROUNDS, pack, 0)

    pick = column(ints[4])
    own_picks = jnp.where(pick == iota((rows, rows), 1), 1.0, 0.0).astype(BF16)
    a_lane = iota((rows, entries), 1)
    got = pick == rows + (a_lane >> 4) * CAP + (a_lane & 3)
    for c in range(4):
        slot_hot[c, :, :rows] = own_picks
        slot_hot[c, :, rows:] = jnp.where(got & (((a_lane >> 2) & 3) == c), 1.0, 0.0).astype(BF16)

    x_copy.wait()
    down_copy.wait()
    down_rows[...] = dot(x_st[...], down_v[...]).astype(BF16)
    send_d[...] = dot(pack_hot[:, :rows], down_rows[...]).astype(BF16).reshape(send_d.shape)
    for axis, o in hops:
        message(ROUNDS, axis, o, send_d, arr_d).start()

    seg_row = ints[5]
    seg_col = column(seg_row)
    allowed = (seg_col == seg_row) & (iota((rows, rows), 0) <= iota((rows, rows), 1))
    bias[...] = jnp.where(allowed, 0.0, -1e30)
    first = jnp.sum(jnp.where(seg_row < seg_col, 1.0, 0.0), axis=1, keepdims=True)
    position = iota((rows, HEAD), 0).astype(F32) - first
    lane = iota((rows, HEAD), 1)
    half = lane % (HEAD // 2)
    frequency = jnp.exp(half.astype(F32) * (-2.0 * math.log(ROPE_THETA) / HEAD))
    angles = position * frequency
    cos_v[...] = jnp.cos(angles)
    sin_v[...] = jnp.where(lane < HEAD // 2, jnp.sin(angles), -jnp.sin(angles))
    lift[...] = jnp.zeros_like(lift)

    def turn(i, carry):
        at = pl.multiple_of(i * HEAD, HEAD)
        x_turned[pl.ds(at, HEAD), :] = jnp.transpose(x_st[:, pl.ds(at, HEAD)])
        return carry

    lax.fori_loop(0, width // HEAD, turn, 0)
    up_copy.wait()

    def remote(src, dst, to_sem, from_sem, to):
        return pltpu.make_async_remote_copy(
            src_ref=src,
            dst_ref=dst,
            send_sem=to_sem,
            recv_sem=from_sem,
            device_id=to,
            device_id_type=pl.DeviceIdType.MESH,
        )

    def sums(own_lift):
        a_rows, b_rows = down_sum.shape[0], up_sum.shape[0]

        slab_rows = 2 * n_group * a_rows

        def up_piece(t, g, at_core):
            part = (t * 2 + g // n_x) * n_local + lax.rem(g, n_x) * 2 + at_core
            return dup_ref[pl.ds(pl.multiple_of(part * b_rows, 16), b_rows), :]

        order = [t for t, _ in far] + [z]
        copies = []
        for t in order:
            slab = dot(x_turned[pl.ds(pl.multiple_of(t * slab_rows, 16), slab_rows), :], own_lift)
            own_part[t] = slab.reshape(2 * n_group, a_rows, slab.shape[1])
            for g in range(n_group):
                send_a[t, g, :a_rows, :] = own_part[t, g * 2 + 1 - core].astype(BF16)
                send_a[t, g, a_rows:, :] = up_piece(t, g, 1 - core).astype(BF16)
            copy = remote(send_a.at[t], recv_a.at[t], sem_a.at[0, t], sem_a.at[1, t], sibling)
            copy.start()
            copies.append(copy)
        for t, copy in zip(order, copies[:]):
            copy.wait_recv()
            for g, to in group:
                got = recv_a[t, g].astype(F32)
                a = own_part[t, g * 2 + core] + got[:a_rows]
                b = up_piece(t, g, core) + got[a_rows:]
                send_b[t, g, :a_rows, :] = a.astype(BF16)
                send_b[t, g, a_rows:, :] = b.astype(BF16)
                out = remote(
                    send_b.at[t, g],
                    recv_b.at[t, own_g],
                    sem_b.at[0, t, g],
                    sem_b.at[1, t, own_g],
                    to,
                )
                out.start()
                copies.append(out)
            got = recv_a[t, own_g].astype(F32)
            mid[t, :a_rows, :] = own_part[t, own_g * 2 + core] + got[:a_rows]
            mid[t, a_rows:, :] = up_piece(t, own_g, core) + got[a_rows:]
        for i, t in enumerate(order):
            total = mid[t]
            for g, to in group:
                remote(
                    send_b.at[t, g], recv_b.at[t, g], sem_b.at[0, t, g], sem_b.at[1, t, g], to
                ).wait_recv()
                total += recv_b[t, g].astype(F32)
            if i < len(far):
                send_c[t] = total.astype(BF16)
                out = remote(
                    send_c.at[t], recv_c.at[z], sem_c.at[0, t], sem_c.at[1, z], far[i][1]
                )
                out.start()
                copies.append(out)
            else:
                last[...] = total
        for t, to in far:
            remote(
                send_c.at[t], recv_c.at[t], sem_c.at[0, t], sem_c.at[1, t], to
            ).wait_recv()
            last[...] += recv_c[t].astype(F32)
        down_sum[...] = last[:a_rows, :] * factor
        up_sum[...] = last[a_rows:, :] * factor
        for copy in copies:
            copy.wait_send()

    scale = 1.0 / math.sqrt(HEAD)
    exp_scale = scale * math.log2(math.e)
    up_row = iota((2 * ADAPTER_RANK, HEAD), 0)

    def cot_copies(j):
        return (
            pltpu.make_async_copy(
                keys_out.at[j],
                cot_hbm.at[:, pl.ds(pl.multiple_of(j * HEAD, HEAD), HEAD)],
                out_sem.at[j, 0],
            ),
            pltpu.make_async_copy(
                vals_out.at[j],
                cot_hbm.at[:, pl.ds(pl.multiple_of(KEY_HEAD_WIDTH + j * HEAD, HEAD), HEAD)],
                out_sem.at[j, 1],
            ),
        )

    def head(r, carry):
        for axis, o in hops:
            arrival(r, axis, o, send.at[r], arr.at[r]).wait_recv()

        @pl.when(r + 2 < ROUNDS)
        def _():
            send_round(r + 2)

        arrived = arr[r].reshape(entries, GQ)
        per = GQ // HEAD
        for c in range(4):
            listed = jnp.concatenate([stage[r, :, c * GQ : (c + 1) * GQ], arrived], axis=0)
            part = dot(slot_hot[c], listed).astype(BF16)
            for i in range(per):
                u, col = divmod(c * per + i, 2 * GROUP + 2)
                piece = part[:, i * HEAD : (i + 1) * HEAD]
                if col >= 2 * GROUP:
                    kvs[u, col - 2 * GROUP] = piece
                    continue
                dst, h = (qs, col) if col < GROUP else (gs, col - GROUP)
                for b in range(rows // block):
                    dst[u, b, h * block : (h + 1) * block, :] = piece[b * block : (b + 1) * block]
        tasks = [(u, b) for b in range(rows // block) for u in range(PAIR)]
        d_keys = [[jnp.zeros((block, HEAD), F32)] * (rows // block) for _ in range(PAIR)]
        d_vals = [[jnp.zeros((block, HEAD), F32)] * (rows // block) for _ in range(PAIR)]

        def products(u, b):
            seen = (b + 1) * block
            return dot_t(kvs[u, 0, :seen, :], qs[u, b]), dot_t(kvs[u, 1, :seen, :], gs[u, b])

        ahead = products(*tasks[0])
        for i, (u, b) in enumerate(tasks):
            scores, prob_grads = ahead
            if i + 1 < len(tasks):
                ahead = products(*tasks[i + 1])
            seen = (b + 1) * block
            mask = bias[:seen, b * block : (b + 1) * block]
            for h in range(GROUP):
                cols = slice(h * block, (h + 1) * block)
                score = scores[:, cols] + mask
                top = jnp.max(score, axis=0, keepdims=True)
                weights = jnp.exp2((score - top) * exp_scale)
                probs = weights * (1.0 / jnp.sum(weights, axis=0, keepdims=True))
                prob_grad = prob_grads[:, cols]
                delta = jnp.sum(probs * prob_grad, axis=0, keepdims=True)
                probs_s[u, b, :seen, cols] = probs.astype(BF16)
                grads_s[u, b, :seen, cols] = (probs * (prob_grad - delta)).astype(BF16)
            d_val = dot(probs_s[u, b, :seen, :], gs[u, b])
            d_key = dot(grads_s[u, b, :seen, :], qs[u, b])
            for t in range(b + 1):
                d_vals[u][t] += d_val[t * block : (t + 1) * block]
                d_keys[u][t] += d_key[t * block : (t + 1) * block]
        total = lift[...]
        for u in range(PAIR):
            j = r * PAIR + u
            d_key = jnp.concatenate(d_keys[u], axis=0) * scale
            d_key = d_key * cos_v[...] + pltpu.roll(d_key, HEAD // 2, 1) * sin_v[...]
            key_low = d_key.astype(BF16)
            val_low = jnp.concatenate(d_vals[u], axis=0).astype(BF16)
            keys_out[j] = key_low
            vals_out[j] = val_low
            up = up_ref[:, pl.ds(pl.multiple_of(j * HEAD, HEAD), HEAD)].astype(F32)
            up_key = jnp.where(up_row < ADAPTER_RANK, up, 0.0).astype(BF16)
            up_val = jnp.where(up_row < ADAPTER_RANK, 0.0, up).astype(BF16)
            total += dot_t(key_low, up_key) + dot_t(val_low, up_val)
        lift[...] = total
        for u in range(PAIR):
            for copy in cot_copies(r * PAIR + u):
                copy.start()
        return carry

    lax.fori_loop(0, ROUNDS, head, 0)

    lift_low = lift[...].astype(BF16)
    send_l[...] = dot_l(slot_hot[0, :, rows:], lift_low).astype(BF16).reshape(send_l.shape)
    for axis, o in hops:
        message(ROUNDS + 1, axis, o, send_l, arr_l).start()

    for axis, o in hops:
        arrival(ROUNDS, axis, o, send_d, arr_d).wait_recv()
    down_out = dot(slot_hot[0, :, :rows], down_rows[...])
    down_out += dot(slot_hot[0, :, rows:], arr_d[...].reshape(entries, HEAD))
    down_low = down_out.astype(BF16)
    down_lane = iota((HEAD, 2 * ADAPTER_RANK), 1) < ADAPTER_RANK

    def up_grad(j, carry):
        from_key = dot_l(keys_out[j], down_low)
        from_val = dot_l(vals_out[j], down_low)
        dup_ref[pl.ds(pl.multiple_of(j * HEAD, HEAD), HEAD), :] = jnp.where(
            down_lane, from_key, from_val
        )
        return carry

    lax.fori_loop(0, KV_HEADS, up_grad, 0)

    own_lift = dot_l(slot_hot[0, :, :rows], lift_low)
    for axis, o in hops:
        arrival(ROUNDS + 1, axis, o, send_l, arr_l).wait_recv()
    own_lift += dot_l(pack_hot[:, :rows], arr_l[...].reshape(entries, HEAD))
    own_lift = own_lift.astype(BF16)
    if factor is None:
        span = width // 8
        for c in range(8):
            at = slice(c * span, (c + 1) * span)
            ddown_ref[at, :] = dot(x_turned[at, :], own_lift)
    else:
        sums(own_lift)

    def finish(j, carry):
        for copy in cot_copies(j):
            copy.wait()
        return carry

    lax.fori_loop(0, KV_HEADS, finish, 0)

    def sent(r, carry):
        for axis, o in hops:
            message(r, axis, o, send.at[r], arr.at[r]).wait_send()
        return carry

    lax.fori_loop(0, ROUNDS, sent, 0)
    for axis, o in hops:
        message(ROUNDS, axis, o, send_d, arr_d).wait_send()
        message(ROUNDS + 1, axis, o, send_l, arr_l).wait_send()


def sum_kernel(
    n_local,
    n_node,
    factor,
    a_ref,
    b_ref,
    a_out,
    b_out,
    send_a,
    recv_a,
    send_b,
    recv_b,
    send_c,
    recv_c,
    mid,
    last,
    sem_a,
    sem_b,
    sem_c,
):
    n_x, n_z = n_local // 2, n_node // 2
    own_l = lax.axis_index("local")
    own_n = lax.axis_index("node")
    core, lx = lax.rem(own_l, 2), own_l // 2
    y, z = lax.rem(own_n, 2), own_n // 2
    a_rows = a_ref.shape[4]
    n_group = 2 * n_x
    own_g = y * n_x + lx
    mesh_id = pl.DeviceIdType.MESH

    sibling = {"local": lx * 2 + (1 - core), "node": own_n}
    group = []
    for o in range(1, n_group):
        g = lax.rem(own_g + o, n_group)
        group.append((g, {"local": lax.rem(g, n_x) * 2 + core, "node": z * 2 + g // n_x}))
    far = []
    for o in range(1, n_z):
        t = lax.rem(z + o, n_z)
        far.append((t, {"local": own_l, "node": t * 2 + y}))

    barrier = pltpu.get_barrier_semaphore()
    targets = [sibling] + [d for _, d in group] + [d for _, d in far]
    for d in targets:
        pl.semaphore_signal(barrier, inc=1, device_id=d, device_id_type=mesh_id)

    for yy in range(2):
        for xx in range(n_x):
            g = yy * n_x + xx
            send_a[g, :, :a_rows, :] = a_ref[:, yy, xx, 1 - core].astype(BF16)
            send_a[g, :, a_rows:, :] = b_ref[:, yy, xx, 1 - core].astype(BF16)
    pl.semaphore_wait(barrier, len(targets))
    copies_a = []
    for o in range(n_group):
        g = lax.rem(own_g + 1 + o, n_group)
        copy = pltpu.make_async_remote_copy(
            src_ref=send_a.at[g],
            dst_ref=recv_a.at[g],
            send_sem=sem_a.at[0, g],
            recv_sem=sem_a.at[1, g],
            device_id=sibling,
            device_id_type=mesh_id,
        )
        copy.start()
        copies_a.append((g, copy))

    copies_b = []
    for o in range(n_group):
        g, copy = copies_a[o]
        copy.wait_recv()
        yy, xx = g // n_x, lax.rem(g, n_x)
        top = a_ref[:, yy, xx, core] + recv_a[g, :, :a_rows, :].astype(F32)
        low = b_ref[:, yy, xx, core] + recv_a[g, :, a_rows:, :].astype(F32)
        if o < n_group - 1:
            send_b[g, :, :a_rows, :] = top.astype(BF16)
            send_b[g, :, a_rows:, :] = low.astype(BF16)
            out = pltpu.make_async_remote_copy(
                src_ref=send_b.at[g],
                dst_ref=recv_b.at[own_g],
                send_sem=sem_b.at[0, g],
                recv_sem=sem_b.at[1, own_g],
                device_id=group[o][1],
                device_id_type=mesh_id,
            )
            out.start()
            copies_b.append(out)
        else:
            mid[:, :a_rows, :] = top
            mid[:, a_rows:, :] = low

    for g, d in group:
        pltpu.make_async_remote_copy(
            src_ref=send_b.at[g],
            dst_ref=recv_b.at[g],
            send_sem=sem_b.at[0, g],
            recv_sem=sem_b.at[1, g],
            device_id=d,
            device_id_type=mesh_id,
        ).wait_recv()
        mid[...] += recv_b[g].astype(F32)

    copies_c = []
    for t, d in far:
        send_c[t] = mid[t].astype(BF16)
        out = pltpu.make_async_remote_copy(
            src_ref=send_c.at[t],
            dst_ref=recv_c.at[z],
            send_sem=sem_c.at[0, t],
            recv_sem=sem_c.at[1, z],
            device_id=d,
            device_id_type=mesh_id,
        )
        out.start()
        copies_c.append(out)
    last[...] = mid[z]
    for t, d in far:
        pltpu.make_async_remote_copy(
            src_ref=send_c.at[t],
            dst_ref=recv_c.at[t],
            send_sem=sem_c.at[0, t],
            recv_sem=sem_c.at[1, t],
            device_id=d,
            device_id_type=mesh_id,
        ).wait_recv()
        last[...] += recv_c[t].astype(F32)
    a_out[...] = last[:a_rows, :] * factor
    b_out[...] = last[a_rows:, :] * factor
    for _, copy in copies_a:
        copy.wait_send()
    for copy in copies_b + copies_c:
        copy.wait_send()


def factor_sums(n_local, n_node, factor, a, b):
    n_x, n_z = n_local // 2, n_node // 2
    n_dev = n_local * n_node

    def lay(v):
        size = v.shape[0] // n_dev
        padded = -(-size // 16) * 16
        v = v.reshape(n_dev, size, v.shape[1])
        if padded != size:
            v = jnp.pad(v, ((0, 0), (0, padded - size), (0, 0)))
        return v.reshape(n_z, 2, n_x, 2, padded, v.shape[2]), size, padded

    a, a_size, a_rows = lay(a)
    b, b_size, b_rows = lay(b)
    rows = a_rows + b_rows
    wide = a.shape[-1]
    n_group = 2 * n_x
    vmem = pl.BlockSpec(memory_space=pltpu.VMEM)
    a_out, b_out = pl.pallas_call(
        functools.partial(sum_kernel, n_local, n_node, factor),
        out_shape=(
            jax.ShapeDtypeStruct((a_rows, wide), F32),
            jax.ShapeDtypeStruct((b_rows, wide), F32),
        ),
        in_specs=[vmem, vmem],
        out_specs=(vmem, vmem),
        scratch_shapes=[
            pltpu.VMEM((n_group, n_z, rows, wide), BF16),
            pltpu.VMEM((n_group, n_z, rows, wide), BF16),
            pltpu.VMEM((n_group, n_z, rows, wide), BF16),
            pltpu.VMEM((n_group, n_z, rows, wide), BF16),
            pltpu.VMEM((n_z, rows, wide), BF16),
            pltpu.VMEM((n_z, rows, wide), BF16),
            pltpu.VMEM((n_z, rows, wide), F32),
            pltpu.VMEM((rows, wide), F32),
            pltpu.SemaphoreType.DMA((2, n_group)),
            pltpu.SemaphoreType.DMA((2, n_group)),
            pltpu.SemaphoreType.DMA((2, n_z)),
        ],
        compiler_params=pltpu.CompilerParams(
            collective_id=1, has_side_effects=True, vmem_limit_bytes=48 * 2**20
        ),
        name="factor_sums",
    )(a, b)
    return a_out[:a_size], b_out[:b_size]


def hand_out_kernel(parts, c_in, a_in, b_in, c_out, a_out, b_out, c_v, a_v, b_v, sem):
    step = c_in.shape[0] // parts
    spans = [(c_in, c_v, c_out, i * step, step) for i in range(parts)]
    spans += [(a_in, a_v, a_out, 0, a_in.shape[0]), (b_in, b_v, b_out, 0, b_in.shape[0])]
    loads, stores = [], []
    for i, (src, mid, dst, at, n) in enumerate(spans):
        rows = slice(at, at + n)
        loads.append(pltpu.make_async_copy(src.at[rows], mid.at[rows], sem.at[0, i]))
        stores.append(pltpu.make_async_copy(mid.at[rows], dst.at[rows], sem.at[1, i]))
    for copy in loads:
        copy.start()
    for first, second in zip(loads, stores):
        first.wait()
        second.start()
    for copy in stores:
        copy.wait()


def hand_out(*arrays):
    parts = 4
    hbm = pl.BlockSpec(memory_space=pl.ANY)
    return pl.pallas_call(
        functools.partial(hand_out_kernel, parts),
        out_shape=tuple(jax.ShapeDtypeStruct(v.shape, v.dtype) for v in arrays),
        in_specs=[hbm] * 3,
        out_specs=(hbm,) * 3,
        scratch_shapes=[pltpu.VMEM(v.shape, v.dtype) for v in arrays]
        + [pltpu.SemaphoreType.DMA((2, parts + 2))],
        compiler_params=pltpu.CompilerParams(vmem_limit_bytes=60 * 2**20),
        name="hand_out",
    )(*arrays)


def local(n_local, n_node, *args):
    activations, queries, rotated_key_value, attention_out_grad, adapter_down, adapter_up = args[:6]
    rows, width = activations.shape
    peers = n_local + n_node
    entries = peers * CHUNK
    vmem = pl.BlockSpec(memory_space=pltpu.VMEM)
    hbm = pl.BlockSpec(memory_space=pl.ANY)
    n_dev = n_local * n_node
    wide = 2 * ADAPTER_RANK
    factor = 1.0 / math.sqrt(rows * n_dev)
    a_rows, b_rows = width // n_dev, KEY_HEAD_WIDTH // n_dev
    fused = a_rows % 16 == 0 and b_rows % 16 == 0
    shrink = n_dev if fused else 1
    extra = []
    if fused:
        n_z, n_group, size = n_node // 2, n_local, a_rows + b_rows
        slab = (n_z, n_group, size, wide)
        extra = [
            pltpu.VMEM((KEY_HEAD_WIDTH, wide), F32),
            pltpu.VMEM(slab, BF16),
            pltpu.VMEM(slab, BF16),
            pltpu.VMEM(slab, BF16),
            pltpu.VMEM(slab, BF16),
            pltpu.VMEM((n_z, size, wide), BF16),
            pltpu.VMEM((n_z, size, wide), BF16),
            pltpu.VMEM((n_z, 2 * n_group, a_rows, wide), F32),
            pltpu.VMEM((n_z, size, wide), F32),
            pltpu.VMEM((size, wide), F32),
            pltpu.SemaphoreType.DMA((2, n_z)),
            pltpu.SemaphoreType.DMA((2, n_z, n_group)),
            pltpu.SemaphoreType.DMA((2, n_z)),
        ]
    cotangent, down_grad, up_grad = pl.pallas_call(
        functools.partial(main_kernel, n_local, n_node, factor if fused else None),
        out_shape=(
            jax.ShapeDtypeStruct((rows, 2 * KEY_HEAD_WIDTH), BF16),
            jax.ShapeDtypeStruct((width // shrink, wide), F32),
            jax.ShapeDtypeStruct((KEY_HEAD_WIDTH // shrink, wide), F32),
        ),
        in_specs=[hbm] * 12,
        out_specs=(hbm, vmem, vmem),
        scratch_shapes=[
            pltpu.VMEM((6, 1, rows), jnp.int32),
            pltpu.VMEM(adapter_up.shape, BF16),
            pltpu.VMEM((ROUNDS, rows, PAIR * GW), BF16),
            pltpu.VMEM((rows, width), BF16),
            pltpu.VMEM((width, rows), BF16),
            pltpu.VMEM((width, 2 * ADAPTER_RANK), BF16),
            pltpu.VMEM((rows, 2 * ADAPTER_RANK), BF16),
            pltpu.VMEM((ROUNDS, peers, CHUNK, GQ), BF16),
            pltpu.VMEM((peers, CHUNK, 2 * ADAPTER_RANK), BF16),
            pltpu.VMEM((peers, CHUNK, 2 * ADAPTER_RANK), BF16),
            pltpu.VMEM((ROUNDS, peers, CHUNK, GQ), BF16),
            pltpu.VMEM((peers, CHUNK, 2 * ADAPTER_RANK), BF16),
            pltpu.VMEM((peers, CHUNK, 2 * ADAPTER_RANK), BF16),
            pltpu.VMEM((entries, 4 * rows), BF16),
            pltpu.VMEM((4, rows, rows + entries), BF16),
            pltpu.VMEM((rows, rows), F32),
            pltpu.VMEM((rows, HEAD), F32),
            pltpu.VMEM((rows, HEAD), F32),
            pltpu.VMEM((PAIR, rows // HEAD, GROUP * HEAD, HEAD), BF16),
            pltpu.VMEM((PAIR, rows // HEAD, GROUP * HEAD, HEAD), BF16),
            pltpu.VMEM((PAIR, 2, rows, HEAD), BF16),
            pltpu.VMEM((PAIR, rows // HEAD, rows, GROUP * HEAD), BF16),
            pltpu.VMEM((PAIR, rows // HEAD, rows, GROUP * HEAD), BF16),
            pltpu.VMEM((KV_HEADS, rows, HEAD), BF16),
            pltpu.VMEM((KV_HEADS, rows, HEAD), BF16),
            pltpu.VMEM((rows, 2 * ADAPTER_RANK), F32),
            pltpu.SemaphoreType.DMA((6,)),
            pltpu.SemaphoreType.DMA((ROUNDS, 4 * PAIR)),
            pltpu.SemaphoreType.DMA((3,)),
            pltpu.SemaphoreType.DMA((KV_HEADS, 2)),
            pltpu.SemaphoreType.DMA((ROUNDS + 2, peers)),
            pltpu.SemaphoreType.DMA((ROUNDS + 2, peers)),
            *extra,
        ],
        compiler_params=pltpu.CompilerParams(
            collective_id=0, has_side_effects=True, vmem_limit_bytes=60 * 2**20
        ),
        name="exchange_attention",
    )(*args)
    if fused:
        return hand_out(cotangent, down_grad, up_grad)
    down_sum, up_sum = factor_sums(n_local, n_node, factor, down_grad, up_grad)
    return cotangent, down_sum, up_sum


def solution(mesh):
    placed = (P(("node", "local"), None),) * 4 + (P(),) * 2 + (P(("node", "local"), None),) * 6
    return jax.shard_map(
        functools.partial(local, mesh.shape["local"], mesh.shape["node"]),
        mesh=mesh,
        in_specs=placed,
        out_specs=(P(("node", "local"), None),) * 3,
        check_vma=False,
    )
```
